32 devices in a mesh: rep: 4 (over y, x), shard: 8 (over z, core).
Axes of the slice: x: 2, y: 2, z: 4, core: 2. Of those that a mesh axis runs over, the one named last changes fastest.
Arguments:
- tokens: bfloat16 [4096, 768], P(('rep', 'shard')), may hold values from -6 to 6
- out_grad: bfloat16 [4096, 768], P(('rep', 'shard')), may hold values from -6 to 6
- lengths: int32 [32, 4], P(('rep', 'shard')), may hold values from 0 to 128, as said below
- gains: bfloat16 [2, 768], P(None, 'shard'), may hold values from 0.5 to 1.5
- shifts: bfloat16 [6, 768], P(None, 'shard'), may hold values from -3 to 3
- w_qkv: bfloat16 [768, 2304], P('shard'), may hold values from -0.21875 to 0.21875
- w_proj: bfloat16 [768, 768], P('shard'), may hold values from -0.875 to 0.875
- w_fc: bfloat16 [768, 3072], P('shard'), may hold values from -0.21875 to 0.21875
- bias_fc: bfloat16 [3072], P('shard'), may hold values from -3 to 3
- w_fc2: bfloat16 [3072, 768], P('shard'), may hold values from -0.109375 to 0.109375
Outputs:
- mixed_out: bfloat16 [4096, 768], P(('rep', 'shard'))
- grad_tokens: float32 [4096, 768], P(('rep', 'shard'))
- grad_gains: float32 [2, 768], P(None, 'shard')
- grad_shifts: float32 [6, 768], P(None, 'shard')
- grad_w_qkv: float32 [768, 2304], P('shard')
- grad_w_proj: float32 [768, 768], P('shard')
- grad_w_fc: float32 [768, 3072], P('shard')
- grad_bias_fc: float32 [3072], P('shard')
- grad_w_fc2: float32 [3072, 768], P('shard')
The draws below stay inside these ranges and needn't reach their ends.
Inputs may be any that keep to these rules, and one draw needn't show every extreme that they name: `lengths`: row d lists, in slot order from slot 0, the sequences on device d = 8 * rep + shard; zeros stand only after the last sequence; the first entry is 1 or more; a row sums to at most 128; some row holds a single sequence of 128.
All inputs are finite; a program needn't handle non-finite values.
Results may differ from the reference program's by a relative error of at most 0.014.
Values may be sent and summed in bfloat16 or wider, within the bound.
No kernel may reach another device: no remote copies, remote signals or barrier semaphores. Data moves between devices by JAX's collectives and lax.ppermute only.
A program may use at most 128 MiB of HBM per device.

```python
import math
import jax
import jax.numpy as jnp
from jax import lax

D = 768
HEADS = 12
HEAD_DIM = 64
FF = 3072
CAP = 128
SEQ_DEV = 4
HOLDERS = 32
SLOTS = 4096


def draw_lengths(key, part):
    key = jax.random.fold_in(key, 11)
    subkeys = jax.random.split(key, 3)
    drawn = jax.random.randint(subkeys[0], (HOLDERS, SEQ_DEV), 1, CAP + 1)
    seq_count = jax.random.randint(subkeys[1], (HOLDERS, 1), 1, SEQ_DEV + 1)
    column = jnp.arange(SEQ_DEV)[None, :]
    drawn = jnp.where(column < seq_count, drawn, 0)
    chosen = jax.random.randint(subkeys[2], (), 0, HOLDERS)
    row_index = jnp.arange(HOLDERS)[:, None]
    drawn = jnp.where((row_index == chosen) & (column == 0), CAP, drawn)
    before = jnp.cumsum(drawn, axis=1) - drawn
    return jnp.clip(jnp.minimum(drawn, CAP - before), 0, CAP).astype(jnp.int32)


def steps_of(own_key, extent, shards, least, largest):
    factor_of = 1.0
    for position, shards_of in shards:
        heights = jax.random.uniform(jax.random.fold_in(jax.random.fold_in(own_key, 6), position), (shards_of,), jnp.float32, least / len(shards), largest / len(shards))
        factor_of = factor_of * jnp.repeat(jnp.exp(heights), extent[position] // shards_of).reshape((-1,) + (1,) * (len(extent) - 1 - position))
    return factor_of


def bell_draw(key, shape, scale, most, cuts=(), held_as=jnp.bfloat16):
    array = jax.random.normal(key, shape, jnp.float32) * scale
    if len(cuts) > 0:
        array = steps_of(key, shape, cuts, -0.22, 0.18) * array
    return jnp.clip(array, min=-most, max=most).astype(held_as)


def setup_inputs(seed: int = 0) -> dict:
    keys = jax.random.split(jax.random.key(seed), 11)
    tokens = bell_draw(keys[0], (SLOTS, D), 1.0, 6.0, ((0, 32),))
    out_grad = bell_draw(keys[1], (SLOTS, D), 1.0, 6.0, ((0, 32),))
    lengths = draw_lengths(jax.random.fold_in(keys[10], 71), 0)
    gains = jnp.clip(1.0 + 0.1 * jax.random.normal(keys[3], (2, D), jnp.float32), 0.5, 1.5).astype(jnp.bfloat16)
    shifts = bell_draw(keys[4], (6, D), 0.5, 3.0, ((1, 8),))
    w_qkv = bell_draw(keys[5], (D, 3 * D), D ** -0.5, 0.21875, ((0, 8),))
    w_proj = bell_draw(keys[6], (D, D), (D // 16) ** -0.5, 0.875, ((0, 8),))
    w_fc = bell_draw(keys[7], (D, FF), D ** -0.5, 0.21875, ((0, 8),))
    bias_fc = bell_draw(keys[8], (FF,), 0.5, 3.0, ((0, 8),))
    w_fc2 = bell_draw(keys[9], (FF, D), FF ** -0.5, 0.109375, ((0, 8),))
    return {"tokens": tokens, "out_grad": out_grad, "lengths": lengths, "gains": gains, "shifts": shifts, "w_qkv": w_qkv, "w_proj": w_proj, "w_fc": w_fc, "bias_fc": bias_fc, "w_fc2": w_fc2}


@jax.custom_vjp
def low(v):
    return lax.optimization_barrier(v.astype(jnp.bfloat16)).astype(jnp.float32)

@jax.custom_vjp
def low_back(v):
    return v

def low_keep(v):
    return (low(v), None)

def low_pass(kept, grad):
    return (grad,)

def back_keep(v):
    return (v, None)

def back_low(kept, grad):
    return (low(grad),)
low.defvjp(low_keep, low_pass)
low_back.defvjp(back_keep, back_low)
EPS = 1e-05
top_precision = lax.Precision.HIGHEST

def normalize(values, gain_row, shift_row):
    row_mean = lax.optimization_barrier(jnp.mean(values, axis=-1, keepdims=True))
    centered = values - row_mean
    variance = lax.optimization_barrier(jnp.mean(centered * centered, axis=-1, keepdims=True))
    return centered * lax.rsqrt(variance + EPS) * gain_row + shift_row

def layout(length_row):
    seq_ends = jnp.cumsum(length_row).astype(jnp.int32)
    place_ids = jnp.arange(CAP, dtype=jnp.int32)
    segment = lax.optimization_barrier(jnp.sum((seq_ends[None, :] <= place_ids[:, None]).astype(jnp.int32), axis=1))
    is_live = place_ids < seq_ends[-1]
    segment = jnp.where(is_live, segment, -1)
    allowed = (segment[:, None] == segment[None, :]) & (place_ids[None, :] <= place_ids[:, None])
    return (is_live, allowed)

def attend(qkv_rows, allowed):
    queries = qkv_rows[:, :D].reshape(CAP, HEADS, HEAD_DIM)
    key_heads = qkv_rows[:, D:2 * D].reshape(CAP, HEADS, HEAD_DIM)
    value_heads = qkv_rows[:, 2 * D:].reshape(CAP, HEADS, HEAD_DIM)
    scores = jnp.einsum('qhd,khd->hqk', queries, key_heads, precision=top_precision) * HEAD_DIM ** (-0.5)
    scores = low_back(scores)
    scores = jnp.where(allowed[None], scores, -1000000000.0)
    row_peak = lax.optimization_barrier(jnp.max(scores, axis=-1, keepdims=True))
    exponent = jnp.exp(scores - row_peak)
    probs = exponent / lax.optimization_barrier(jnp.sum(exponent, axis=-1, keepdims=True))
    probs = low(probs)
    attended = jnp.einsum('hqk,khd->qhd', probs, value_heads, precision=top_precision)
    return attended.reshape(CAP, D)

def block_layer(params, block_rows, allowed):
    gains, shifts, w_qkv, w_proj, w_fc, bias_fc, w_fc2 = params
    normed_one = low(normalize(block_rows, gains[0], shifts[0]))
    qkv_bias = jnp.concatenate([shifts[2], jnp.zeros_like(shifts[2]), shifts[3]])
    qkv = jnp.einsum('gtd,de->gte', normed_one, w_qkv, precision=top_precision) + qkv_bias
    qkv = low(low_back(qkv))
    attended = jax.vmap(jax.checkpoint(attend))(qkv, allowed)
    attended = low(low_back(attended))
    branch = low_back(jnp.einsum('gtd,de->gte', attended, w_proj, precision=top_precision) + shifts[4])
    middle = block_rows + branch
    normed_two = low(normalize(middle, gains[1], shifts[1]))
    hidden = low_back(jnp.einsum('gtd,de->gte', normed_two, w_fc, precision=top_precision) + bias_fc)
    active = low(jax.nn.gelu(hidden, approximate=True))
    result = low_back(jnp.einsum('gtf,fd->gtd', active, w_fc2, precision=top_precision) + shifts[5])
    return middle + result

def reference(tokens, out_grad, lengths, gains, shifts, w_qkv, w_proj, w_fc, bias_fc, w_fc2):
    params = (gains.astype(jnp.float32), shifts.astype(jnp.float32), w_qkv.astype(jnp.float32), w_proj.astype(jnp.float32), w_fc.astype(jnp.float32), bias_fc.astype(jnp.float32), w_fc2.astype(jnp.float32))
    group_size = math.gcd(HOLDERS, max(1, 4096 // CAP))
    step_count = HOLDERS // group_size
    token_rows = tokens.astype(jnp.float32).reshape(step_count, group_size, CAP, D)
    cotangent = out_grad.astype(jnp.float32).reshape(step_count, group_size, CAP, D)
    length_rows = lengths.reshape(step_count, group_size, SEQ_DEV)

    def scan_step(running, inputs):
        block_rows, block_cot, block_lengths = inputs
        is_live, allowed = jax.vmap(layout)(block_lengths)
        live_f = is_live.astype(jnp.float32)[..., None]

        def apply_layer(param_set, rows_in):
            return block_layer(param_set, rows_in, allowed)
        result, pull_back = jax.vjp(apply_layer, params, block_rows)
        grad_params, grad_rows = pull_back(block_cot * live_f)
        running = jax.tree.map(lambda total_part, extra_part: total_part + extra_part, running, grad_params)
        return (running, ((result * live_f).astype(jnp.bfloat16), grad_rows))
    initial = tuple((jnp.zeros(param_entry.shape, jnp.float32) for param_entry in params))
    summed, outputs = lax.scan(scan_step, initial, (token_rows, cotangent, length_rows))
    mixed_rows, grad_rows = outputs
    return (mixed_rows.reshape(SLOTS, D), grad_rows.reshape(SLOTS, D), summed[0], summed[1], summed[2], summed[3], summed[4], summed[5], summed[6])
```

```python
from functools import partial

import jax
import jax.numpy as jnp
from jax import lax
from jax.experimental import pallas as pl
from jax.experimental.pallas import tpu as pltpu
from jax.sharding import PartitionSpec as P

HEAD_DIM = 64
EPS = 1e-05
LOW = jnp.bfloat16
F32 = jnp.float32


def normalize(values, gain_row, shift_row):
    row_mean = jnp.mean(values, axis=-1, keepdims=True)
    centered = values - row_mean
    variance = jnp.mean(centered * centered, axis=-1, keepdims=True)
    return centered * lax.rsqrt(variance + EPS) * gain_row + shift_row


def layout(length_row, slot_count):
    seq_ends = jnp.cumsum(length_row)
    place_ids = jnp.arange(slot_count, dtype=jnp.int32)
    segment = jnp.sum((seq_ends[None, :] <= place_ids[:, None]).astype(jnp.int32), axis=1)
    is_live = place_ids < seq_ends[-1]
    segment = jnp.where(is_live, segment, -1)
    allowed = (segment[:, None] == segment[None, :]) & (place_ids[None, :] <= place_ids[:, None])
    return (is_live, allowed)


def contract(left_rows, right_rows):
    return lax.dot_general(
        left_rows, right_rows, (((0,), (0,)), ((), ())), preferred_element_type=F32
    )


def back_mult(grad_rows, weight):
    return lax.dot_general(
        grad_rows, weight, (((1,), (1,)), ((), ())), preferred_element_type=F32
    )


class Links:
    def __init__(self):
        self.shards = lax.axis_size("shard")
        self.line = self.shards // 2
        place = lax.axis_index("shard")
        self.z = place // 2
        self.c = place % 2
        self.j = lax.axis_index("rep")
        assert lax.axis_size("rep") == 4

    def core(self, v):
        return lax.ppermute(v, "shard", [(i, i ^ 1) for i in range(self.shards)])

    def along(self, v, hop):
        n = self.shards
        return lax.ppermute(v, "shard", [(i, (i + 2 * hop) % n) for i in range(n)])

    def rep(self, v, k):
        return lax.ppermute(v, "rep", [(i, i ^ k) for i in range(4)])

    def rep_gather(self, v):
        return [v] + [self.rep(v, k) for k in range(1, 4)]

    def rep_sum(self, parts):
        total = parts[0]
        for k in range(1, 4):
            total = total + self.rep(parts[k].astype(LOW), k).astype(F32)
        return total


def pick(stack, index, axis=0):
    return lax.dynamic_index_in_dim(stack, index, axis, keepdims=False)


def line_gather(links, block, sizes):
    line = links.line
    mine = [block] + [links.along(block, hop) for hop in range(1, line)]
    theirs = links.core(jnp.stack(mine))
    scalars = jnp.stack([links.z, links.c]).astype(jnp.int32)
    width = block.shape[1]

    def kernel(scalar_ref, *refs):
        ins, partner, outs = refs[:line], refs[line], refs[line + 1 :]
        z, c = scalar_ref[0], scalar_ref[1]
        for hop in range(line):
            at = lax.rem(z + line - hop, line)
            start = 0
            for size, out in zip(sizes, outs):
                out[at, c] = ins[hop][pl.ds(start, size), :]
                out[at, 1 - c] = partner[hop, pl.ds(start, size), :]
                start += -(-size // 16) * 16

    return pl.pallas_call(
        kernel,
        out_shape=[jax.ShapeDtypeStruct((line, 2, size, width), LOW) for size in sizes],
        in_specs=[pl.BlockSpec(memory_space=pltpu.SMEM)]
        + [pl.BlockSpec(memory_space=pltpu.VMEM)] * (line + 1),
        out_specs=[pl.BlockSpec(memory_space=pltpu.VMEM)] * len(sizes),
        compiler_params=pltpu.CompilerParams(vmem_limit_bytes=48 * 1024 * 1024),
    )(scalars, *mine, theirs)


def line_scatter(links, grads):
    line = links.line
    theirs = links.core(pick(grads, 1 - links.c, 1))
    both = pick(grads, links.c, 1).astype(F32) + theirs.astype(F32)
    low = both.astype(LOW)
    total = pick(both, links.z)
    for hop in range(1, line):
        sent = pick(low, (links.z + hop) % line)
        total = total + links.along(sent, hop).astype(F32)
    return total


def pad_rows(v, rows):
    return v if v.shape[0] == rows else jnp.pad(v, ((0, rows - v.shape[0]), (0, 0)))


def local(tokens, out_grad, lengths, gains, shifts, w_qkv, w_proj, w_fc, bias_fc, w_fc2):
    links = Links()
    line, shards = links.line, links.shards
    z, c, j = links.z, links.c, links.j
    slots, model = tokens.shape
    rows = w_proj.shape[0]
    quarter = w_fc2.shape[0] // 4
    ff = 4 * model
    assert quarter == rows and w_fc.shape[1] == ff
    heads = model // HEAD_DIM // 4
    part = heads * HEAD_DIM
    scale = HEAD_DIM ** (-0.5)
    full_rows = -(-rows // 16) * 16
    extra = -(-9 * rows // model)

    lengths_row = jnp.pad(lengths.astype(LOW), ((0, 0), (0, model - lengths.shape[1])))
    tokens_sent = jnp.concatenate([tokens, lengths_row])
    bias_part = lax.dynamic_slice_in_dim(bias_fc, j * quarter, quarter)
    small = jnp.concatenate([gains, shifts, bias_part[None]]).reshape(-1)
    small = jnp.pad(small, (0, extra * model - small.shape[0])).reshape(extra, model)
    thirds = [
        lax.dynamic_slice_in_dim(w_qkv, third * model + j * part, part, 1) for third in range(3)
    ]
    proj_part = lax.dynamic_slice_in_dim(w_proj, j * part, part, 1)
    attn_block = jnp.concatenate(thirds + [proj_part], axis=1)
    attn_block = jnp.concatenate([pad_rows(attn_block, full_rows), small])
    fc_block = pick(w_fc.reshape(rows, shards, 4, quarter), j, 2).reshape(rows, model)
    fc2_block = lax.dynamic_slice_in_dim(w_fc2, j * quarter, quarter, 0)
    ff_block = jnp.concatenate([pad_rows(fc_block, full_rows), fc2_block])

    attn_full, small_full = line_gather(links, attn_block, [rows, extra])
    tokens_got = jnp.stack(links.rep_gather(tokens_sent))
    fc_full, fc2_full = line_gather(links, ff_block, [rows, quarter])
    cot_got = jnp.stack(links.rep_gather(out_grad))

    attn_full = attn_full.reshape(model, model)
    fc_full = fc_full.reshape(model, model)
    fc2_full = fc2_full.reshape(model, model)
    small_full = small_full.reshape(shards, extra * model)[:, : 9 * rows]
    small_full = small_full.reshape(shards, 9, rows).transpose(1, 0, 2).reshape(9, model)
    small_full = small_full.astype(F32)
    gain_f, shift_f, bias_f = small_full[:2], small_full[2:8], small_full[8]

    inputs_f = tokens_got[:, :slots].astype(F32)
    lengths_got = tokens_got[:, slots, : lengths.shape[1]].astype(jnp.int32)
    is_live, allowed = jax.vmap(partial(layout, slot_count=slots))(lengths_got)
    live_f = is_live.astype(F32)[..., None]
    grad_out = cot_got.astype(F32) * live_f
    grad_out_low = grad_out.astype(LOW).reshape(4 * slots, model)

    normed_one = normalize(inputs_f, gain_f[0], shift_f[0]).astype(LOW).reshape(4 * slots, model)
    qkv_w = attn_full[:, : 3 * part]
    zero = jnp.zeros((part,), F32)
    q_bias = lax.dynamic_slice_in_dim(shift_f[2], j * part, part)
    v_bias = lax.dynamic_slice_in_dim(shift_f[3], j * part, part)
    qkv_bias = jnp.concatenate([q_bias, zero, v_bias])
    qkv_low = (jnp.dot(normed_one, qkv_w, preferred_element_type=F32) + qkv_bias).astype(LOW)
    qkv_low = qkv_low.reshape(4, slots, 3, heads, HEAD_DIM)
    queries, key_heads, value_heads = qkv_low[:, :, 0], qkv_low[:, :, 1], qkv_low[:, :, 2]
    scores = jnp.einsum("bqhd,bkhd->bhqk", queries, key_heads, preferred_element_type=F32)
    scores = jnp.where(allowed[:, None], scores * scale, -1000000000.0)
    row_peak = jnp.max(scores, axis=-1, keepdims=True)
    exponent = jnp.exp(scores - row_peak)
    probs = exponent / jnp.sum(exponent, axis=-1, keepdims=True)
    probs_low = probs.astype(LOW)
    attended = jnp.einsum("bhqk,bkhd->bqhd", probs_low, value_heads, preferred_element_type=F32)
    attended = attended.astype(LOW).reshape(4, slots, part)
    sent = attended.transpose(1, 0, 2).reshape(slots, 4 * part)
    got = links.rep_gather(sent)
    got = [v.reshape(slots, 4, part) for v in got]
    attended_full = jnp.stack(
        [jnp.concatenate([got[m][:, k ^ m] for m in range(4)], axis=1) for k in range(4)]
    ).reshape(4 * slots, model)

    proj_got = jnp.stack(links.rep_gather(attn_full[:, 3 * part :]))
    proj_full = jnp.concatenate([pick(proj_got, j ^ p) for p in range(4)], axis=1)
    proj_rel = jnp.concatenate(
        [lax.dynamic_slice_in_dim(proj_full, (j ^ m) * part, part, 0) for m in range(4)]
    )
    middle = (
        inputs_f.reshape(4 * slots, model)
        + jnp.dot(attended_full, proj_rel, preferred_element_type=F32)
        + shift_f[4]
    )
    normed_two = normalize(middle, gain_f[1], shift_f[1]).astype(LOW)
    hidden = jnp.dot(normed_two, fc_full, preferred_element_type=F32) + bias_f
    gelu_value, gelu_pull = jax.vjp(partial(jax.nn.gelu, approximate=True), hidden)
    active = gelu_value.astype(LOW)
    grad_active = back_mult(grad_out_low, fc2_full)
    grad_hidden = gelu_pull(grad_active)[0].astype(LOW)
    grad_normed_two = links.rep_sum(list(back_mult(grad_hidden, fc_full).reshape(4, slots, model)))

    branch = jnp.dot(active, fc2_full, preferred_element_type=F32).reshape(4, slots, model)
    result = links.rep_sum(list(branch)) + middle[:slots] + shift_f[5]
    mixed_out = (result * live_f[0]).astype(LOW)

    grad_w_fc2 = contract(active, grad_out_low).astype(LOW)
    grad_w_fc = contract(normed_two, grad_hidden).astype(LOW)
    ff_grads = jnp.concatenate(
        [
            grad_w_fc.reshape(line, 2, rows, model),
            grad_w_fc2.reshape(line, 2, quarter, model),
        ],
        axis=2,
    )
    ff_sum = line_scatter(links, ff_grads)

    norm_value, norm_pull = jax.vjp(normalize, middle[:slots], gain_f[1], shift_f[1])
    grad_middle_norm, grad_gain_two, grad_shift_two = norm_pull(grad_normed_two)
    grad_middle = grad_out[0] + grad_middle_norm
    grad_branch_own = grad_middle.astype(LOW)
    grad_branch = jnp.concatenate(links.rep_gather(grad_branch_own))

    grad_proj = contract(
        attended_full, lax.dynamic_slice_in_dim(grad_branch, j * part, part, 1)
    ).astype(LOW)
    grad_proj = jnp.concatenate([pick(grad_proj.reshape(4, part, part), j ^ p) for p in range(4)])
    grad_attended = back_mult(grad_branch, proj_rel[:part]).astype(LOW)
    grad_attended = grad_attended.reshape(4, slots, heads, HEAD_DIM)
    grad_probs = jnp.einsum(
        "bqhd,bkhd->bhqk", grad_attended, value_heads, preferred_element_type=F32
    )
    grad_values = jnp.einsum(
        "bhqk,bqhd->bkhd", probs_low, grad_attended, preferred_element_type=F32
    )
    row_inner = jnp.sum(probs * grad_probs, axis=-1, keepdims=True)
    grad_scores = (probs * (grad_probs - row_inner)).astype(LOW)
    grad_queries = (
        jnp.einsum("bhqk,bkhd->bqhd", grad_scores, key_heads, preferred_element_type=F32) * scale
    )
    grad_keys = (
        jnp.einsum("bhqk,bqhd->bkhd", grad_scores, queries, preferred_element_type=F32) * scale
    )
    grad_qkv = jnp.concatenate(
        [v.reshape(4 * slots, part).astype(LOW) for v in (grad_queries, grad_keys, grad_values)],
        axis=1,
    )
    grad_w_qkv = contract(normed_one, grad_qkv).astype(LOW)
    grad_normed_one = back_mult(grad_qkv, qkv_w)

    qkv_sums = jnp.sum(grad_qkv.astype(F32), axis=0)
    spread = lambda v: lax.dynamic_update_slice_in_dim(jnp.zeros((model,), F32), v, j * part, 0)
    flat_in = inputs_f.reshape(4 * slots, model)
    unit_one = normalize(flat_in, 1.0, 0.0)
    vectors = jnp.stack(
        [
            jnp.sum(grad_normed_one * unit_one, axis=0),
            grad_gain_two,
            jnp.sum(grad_normed_one, axis=0),
            grad_shift_two,
            spread(qkv_sums[:part]),
            spread(qkv_sums[2 * part :]),
            jnp.sum(grad_branch_own.astype(F32), axis=0),
            jnp.sum(grad_out[0], axis=0),
            jnp.sum(grad_hidden.astype(F32), axis=0),
        ]
    )
    vectors = vectors.reshape(9, shards, rows).transpose(1, 0, 2).reshape(shards, 9 * rows)
    vectors = jnp.pad(vectors, ((0, 0), (0, extra * model - 9 * rows)))
    attn_grads = jnp.concatenate(
        [
            jnp.concatenate([grad_w_qkv, grad_proj], axis=1).reshape(line, 2, rows, model),
            vectors.astype(LOW).reshape(line, 2, extra, model),
        ],
        axis=2,
    )
    attn_sum = line_scatter(links, attn_grads)

    grad_normed_one_own = links.rep_sum(list(grad_normed_one.reshape(4, slots, model)))
    first_value, first_pull = jax.vjp(normalize, inputs_f[0], gain_f[0], shift_f[0])
    grad_tokens = grad_middle + first_pull(grad_normed_one_own)[0]

    def ordered(v):
        stacked = jnp.stack(links.rep_gather(v))
        return [pick(stacked, j ^ p) for p in range(4)]

    ff_out = ordered(ff_sum.astype(LOW))
    attn_out = ordered(attn_sum.astype(LOW))
    grad_qkv_out = jnp.concatenate(
        [v[:rows, t * part : (t + 1) * part] for t in range(3) for v in attn_out], axis=1
    )
    grad_proj_out = jnp.concatenate([v[:rows, 3 * part :] for v in attn_out], axis=1)
    sums = [v[rows:].reshape(-1)[: 9 * rows].reshape(9, rows).astype(F32) for v in attn_out]
    eight = (sums[0] + sums[1] + sums[2] + sums[3])[:8]
    bias_out = jnp.concatenate([v[8] for v in sums])
    fc_out = jnp.stack([v[:rows].reshape(rows, shards, quarter) for v in ff_out], axis=2)
    return (
        mixed_out,
        grad_tokens,
        eight[:2],
        eight[2:],
        grad_qkv_out.astype(F32),
        grad_proj_out.astype(F32),
        fc_out.reshape(rows, ff).astype(F32),
        bias_out,
        jnp.concatenate([v[rows:] for v in ff_out]).astype(F32),
    )


def solution(mesh):
    return jax.shard_map(
        local,
        mesh=mesh,
        in_specs=(
            P(("rep", "shard"), None),
            P(("rep", "shard"), None),
            P(("rep", "shard"), None),
            P(None, "shard"),
            P(None, "shard"),
            P("shard", None),
            P("shard", None),
            P("shard", None),
            P("shard"),
            P("shard", None),
        ),
        out_specs=(
            P(("rep", "shard"), None),
            P(("rep", "shard"), None),
            P(None, "shard"),
            P(None, "shard"),
            P("shard", None),
            P("shard", None),
            P("shard", None),
            P("shard"),
            P("shard", None),
        ),
        check_vma=False,
    )
```

```python
from functools import partial

import jax
import jax.numpy as jnp
from jax import lax
from jax.experimental import pallas as pl
from jax.experimental.pallas import tpu as pltpu
from jax.sharding import PartitionSpec as P

HEAD_DIM = 64
EPS = 1e-05
LOW = jnp.bfloat16
F32 = jnp.float32


def normalize(values, gain_row, shift_row):
    row_mean = jnp.mean(values, axis=-1, keepdims=True)
    centered = values - row_mean
    variance = jnp.mean(centered * centered, axis=-1, keepdims=True)
    return centered * lax.rsqrt(variance + EPS) * gain_row + shift_row


def contract(left_rows, right_rows):
    return lax.dot_general(
        left_rows, right_rows, (((0,), (0,)), ((), ())), preferred_element_type=F32
    )


def back_mult(grad_rows, weight):
    return lax.dot_general(
        grad_rows, weight, (((1,), (1,)), ((), ())), preferred_element_type=F32
    )


def mult(left, right):
    return jnp.dot(left, right, preferred_element_type=F32)


class Links:
    def __init__(self):
        self.shards = lax.axis_size("shard")
        self.line = self.shards // 2
        place = lax.axis_index("shard")
        self.z = place // 2
        self.c = place % 2
        self.j = lax.axis_index("rep")
        self.scalars = jnp.stack([self.z, self.c, self.j]).astype(jnp.int32)
        assert lax.axis_size("rep") == 4

    def core(self, v):
        return lax.ppermute(v, "shard", [(i, i ^ 1) for i in range(self.shards)])

    def along(self, v, hop):
        n = self.shards
        return lax.ppermute(v, "shard", [(i, (i + 2 * hop) % n) for i in range(n)])

    def rep(self, v, k):
        return lax.ppermute(v, "rep", [(i, i ^ k) for i in range(4)])

    def rep_gather(self, v):
        return [v] + [self.rep(v, k) for k in range(1, 4)]


def pick(stack, index, axis=0):
    return lax.dynamic_index_in_dim(stack, index, axis, keepdims=False)


def run(kernel, out_shapes, scalars, args, scratch=()):
    return pl.pallas_call(
        kernel,
        out_shape=[jax.ShapeDtypeStruct(shape, dtype) for shape, dtype in out_shapes],
        in_specs=[pl.BlockSpec(memory_space=pltpu.SMEM)]
        + [pl.BlockSpec(memory_space=pltpu.VMEM)] * len(args),
        out_specs=[pl.BlockSpec(memory_space=pltpu.VMEM)] * len(out_shapes),
        scratch_shapes=list(scratch),
        compiler_params=pltpu.CompilerParams(vmem_limit_bytes=56 * 1024 * 1024),
        cost_estimate=pl.CostEstimate(flops=1, bytes_accessed=1, transcendentals=0),
    )(scalars, *args)


def tie(value, *others):
    return lax.optimization_barrier((value, others))[0]


def line_gather(links, block):
    return [block] + [links.along(block, hop) for hop in range(1, links.line)]


def with_partners(links, mine):
    return mine + [links.core(v) for v in mine]


def assemble(scalar_ref, refs, out, start, rows):
    line = len(refs) // 2
    z, c = scalar_ref[0], scalar_ref[1]
    for hop in range(line):
        at = lax.rem(z + line - hop, line)
        for side in range(2):
            to = (2 * at + c) if side == 0 else (2 * at + 1 - c)
            block = refs[side * line + hop][pl.ds(start, rows), :]
            if rows % 16 == 0:
                out[pl.ds(pl.multiple_of(to * rows, 16), rows), :] = block
                continue
            for s in range(2 * line):

                @pl.when(to == s)
                def _(block=block, s=s):
                    out[s * rows : (s + 1) * rows, :] = block


def one_of_pair(scratch, z, side, rows):
    if rows % 16 == 0:
        return scratch[pl.ds(pl.multiple_of((2 * z + side) * rows, 16), rows), :].astype(LOW)
    first, second = (scratch[(2 * z + k) * rows : (2 * z + k + 1) * rows, :] for k in range(2))
    return jnp.where(side == 0, first, second).astype(LOW)


def line_sum(links, mine, theirs):
    line = links.line
    theirs = theirs.astype(F32)
    sent = []
    for hop in range(1, line):
        at = (links.z + hop) % line
        sent.append((pick(mine, at).astype(F32) + pick(theirs, at)).astype(LOW))
    own = pick(mine, links.z).astype(F32) + pick(theirs, links.z)
    return sent, own


def line_send(links, sent, own):
    for hop, value in enumerate(sent, start=1):
        own = own + links.along(value, hop).astype(F32)
    return own


def pad_rows(v, rows):
    return v if v.shape[0] == rows else jnp.pad(v, ((0, rows - v.shape[0]), (0, 0)))


def unit(values):
    row_mean = jnp.mean(values, axis=-1, keepdims=True)
    centered = values - row_mean
    variance = jnp.mean(centered * centered, axis=-1, keepdims=True)
    scale = lax.rsqrt(variance + EPS)
    return centered * scale, scale


def norm_back(cotangent, gain, unit_rows, scale):
    weighted = cotangent * gain
    return scale * (
        weighted
        - jnp.mean(weighted, axis=-1, keepdims=True)
        - unit_rows * jnp.mean(weighted * unit_rows, axis=-1, keepdims=True)
    )


def gelu_pair(x):
    root = 0.7978845608028654
    square = x * x
    bend = jnp.tanh(root * x * (1.0 + 0.044715 * square))
    half = 0.5 * (1.0 + bend)
    slope = half + 0.5 * x * (1.0 - bend * bend) * root * (1.0 + 3 * 0.044715 * square)
    return x * half, slope


def choose(index, options):
    value = options[0]
    for k in range(1, len(options)):
        value = jnp.where(index == k, options[k], value)
    return value


def live_rows(got, slots, count):
    total = jnp.zeros((1, 1), F32)
    for s in range(count):
        total = total + got[2 * slots : 2 * slots + 1, s : s + 1].astype(F32)
    place = lax.broadcasted_iota(jnp.int32, (slots, 1), 0).astype(F32)
    return (place < total).astype(F32)


def pack_attn(links, place, args, slots, rows, part, full):
    tokens, out_grad, lengths, gains, shifts, bias, w_qkv, w_proj = args
    model = tokens.shape[1]
    count = lengths.shape[1]

    def kernel(scalar_ref, tok, cot, len_ref, gain, shift, bias_ref, qkv_ref, p_ref, out, sent):
        j, s_here = scalar_ref[2], scalar_ref[3]
        for t in range(3):
            out[pl.ds(0, rows), t * part : (t + 1) * part] = choose(
                j,
                [
                    qkv_ref[:, t * model + p * part : t * model + (p + 1) * part]
                    for p in range(4)
                ],
            )
        out[pl.ds(0, rows), 3 * part :] = choose(
            j, [p_ref[:, p * part : (p + 1) * part] for p in range(4)]
        )
        mine = choose(j, [bias_ref[:, p * rows : (p + 1) * rows] for p in range(4)])
        small = jnp.concatenate(
            [v.astype(F32) for v in (gain[...], shift[...], mine)] + [jnp.zeros((7, rows), F32)]
        )
        small = jnp.concatenate([small] * links.shards, axis=1)
        lane = lax.broadcasted_iota(jnp.int32, small.shape, 1)
        here = (lane >= s_here * rows) & (lane < (s_here + 1) * rows)
        out[pl.ds(full, 16), :] = jnp.where(here, small, 0.0).astype(LOW)
        sent[pl.ds(0, slots), :] = tok[...]
        sent[pl.ds(slots, slots), :] = cot[...]
        sent[pl.ds(2 * slots, 16), :] = jnp.zeros((16, model), LOW)
        sent[2 * slots : 2 * slots + 1, :count] = len_ref[...].astype(F32).astype(LOW)

    scalars = jnp.concatenate([links.scalars, place[None].astype(jnp.int32)])
    shapes = [((full + 16, model), LOW), ((2 * slots + 16, model), LOW)]
    return run(kernel, shapes, scalars, args)


def pack_ff(links, w_fc, w_fc2, rows, full):
    model = w_fc2.shape[1]

    def kernel(scalar_ref, fc_ref, fc2_ref, out):
        j = scalar_ref[2]
        for s in range(links.shards):
            out[pl.ds(0, rows), s * rows : (s + 1) * rows] = choose(
                j,
                [fc_ref[:, (4 * s + p) * rows : (4 * s + p + 1) * rows] for p in range(4)],
            )
        out[pl.ds(full, rows), :] = choose(
            j, [fc2_ref[p * rows : (p + 1) * rows, :] for p in range(4)]
        )

    return run(kernel, [((full + rows, model), LOW)], links.scalars, [w_fc, w_fc2])[0]


def proj_lanes(links, blocks, rows, part):
    model = blocks[0].shape[1]
    line = links.line

    def kernel(scalar_ref, *refs):
        ins, out, scratch = refs[:-2], refs[-2], refs[-1]
        assemble(scalar_ref, [ref.at[:, pl.ds(512, 256)] for ref in ins], scratch, 0, rows)
        for g in range(4):
            out[:, g * part : (g + 1) * part] = scratch[pl.ds(g * part, part), 64:]

    return run(
        kernel, [((part, model), LOW)], links.scalars, blocks, [pltpu.VMEM((model, 256), LOW)]
    )[0]


def attn_forward(links, got, blocks, slots, heads, count, rows):
    model = blocks[0].shape[1]
    part = heads * HEAD_DIM
    full = -(-rows // 16) * 16

    def kernel(scalar_ref, *refs):
        ins, parts = refs[:4], refs[4 : 4 + len(blocks)]
        w_ref, unit_out, qkv_out, probs_out, sent_out, small_out = refs[4 + len(blocks) :]
        j = scalar_ref[2]
        assemble(scalar_ref, parts, w_ref, 0, rows)
        small_sum = jnp.zeros(small_out.shape, F32)
        for ref in parts:
            small_sum = small_sum + ref[pl.ds(full, 16), :].astype(F32)
        small_out[...] = small_sum
        cut = lambda row: choose(
            j, [small_sum[row : row + 1, p * part : (p + 1) * part] for p in range(4)]
        )
        q_bias, v_bias = cut(4), cut(5)
        rows_at = lax.broadcasted_iota(jnp.int32, (slots, slots), 0).astype(F32)
        cols_at = lax.broadcasted_iota(jnp.int32, (slots, slots), 1).astype(F32)
        for k in range(4):
            normed = unit(ins[k][:slots].astype(F32))[0] * small_sum[0:1] + small_sum[2:3]
            normed = normed.astype(LOW)
            unit_out[k] = normed
            qkv = mult(normed, w_ref[:, : 3 * part])
            qkv_out[k, :, :part] = (qkv[:, :part] + q_bias).astype(LOW)
            qkv_out[k, :, part : 2 * part] = qkv[:, part : 2 * part].astype(LOW)
            qkv_out[k, :, 2 * part :] = (qkv[:, 2 * part :] + v_bias).astype(LOW)
            end = jnp.zeros((1, 1), F32)
            row_seq, col_seq = jnp.zeros((slots, slots), F32), jnp.zeros((slots, slots), F32)
            for s in range(count):
                end = end + ins[k][2 * slots : 2 * slots + 1, s : s + 1].astype(F32)
                row_seq = row_seq + (end <= rows_at).astype(F32)
                col_seq = col_seq + (end <= cols_at).astype(F32)
            allowed = (row_seq == col_seq) & (cols_at <= rows_at)
            for h in range(heads):
                at = h * HEAD_DIM
                query = qkv_out[k, :, at : at + HEAD_DIM]
                keys = qkv_out[k, :, part + at : part + at + HEAD_DIM]
                values = qkv_out[k, :, 2 * part + at : 2 * part + at + HEAD_DIM]
                scores = back_mult(query, keys) * (HEAD_DIM**-0.5)
                scores = jnp.where(allowed, scores, -1000000000.0)
                exponent = jnp.exp(scores - jnp.max(scores, axis=-1, keepdims=True))
                probs = exponent / jnp.sum(exponent, axis=-1, keepdims=True)
                probs_out[k, h] = probs
                attended = mult(probs.astype(LOW), values)
                sent_out[:, k * part + at : k * part + at + HEAD_DIM] = attended.astype(LOW)

    shapes = [
        ((model, model), LOW),
        ((4, slots, model), LOW),
        ((4, slots, 3 * part), LOW),
        ((4, heads, slots, slots), F32),
        ((slots, 4 * part), LOW),
        ((16, model), F32),
    ]
    return run(kernel, shapes, links.scalars, [*got, *blocks])


def ff_both(links, got, attended, proj, blocks, small, slots, count, rows):
    model = blocks[0].shape[1]
    part = model // 4
    full = -(-rows // 16) * 16
    held = 4 + 1 + 4 + len(blocks) + 1

    def kernel(scalar_ref, *refs):
        ins, att, p_parts, parts, small_ref = (
            refs[:4],
            refs[4],
            refs[5:9],
            refs[9 : held - 1],
            refs[held - 1],
        )
        att_out, middle_out, normed_out, active_out, hidden_out, cot_out = refs[held : held + 6]
        own_out, *sent_out = refs[held + 6 : held + 10]
        sums_out, p_ref, fc2_ref, fc_ref = refs[held + 10 :]
        j = scalar_ref[2]
        assemble(scalar_ref, parts, fc_ref, 0, rows)
        assemble(scalar_ref, parts, fc2_ref, full, rows)
        for p in range(4):
            for g in range(4):
                p_ref[pl.ds(g * part, part), p * part : (p + 1) * part] = choose(
                    j ^ p, [ref[:, g * part : (g + 1) * part] for ref in p_parts]
                )
        total = jnp.zeros((1, model), F32)
        for k in range(4):
            for p in range(4):
                att_out[k, :, p * part : (p + 1) * part] = choose(
                    j ^ p, [att[p, :, (k ^ m) * part : ((k ^ m) + 1) * part] for m in range(4)]
                )
            middle = ins[k][:slots].astype(F32) + mult(att_out[k], p_ref[...]) + small_ref[6:7]
            if k == 0:
                middle_out[...] = middle
            normed = (unit(middle)[0] * small_ref[1:2] + small_ref[3:4]).astype(LOW)
            normed_out[k] = normed
            hidden = mult(normed, fc_ref[...]) + small_ref[8:9]
            active, slope = gelu_pair(hidden)
            active_out[k] = active.astype(LOW)
            live = live_rows(ins[k], slots, count)
            cot = (ins[k][slots : 2 * slots].astype(F32) * live).astype(LOW)
            cot_out[k] = cot
            grad_hidden = (back_mult(cot, fc2_ref[...]) * slope).astype(LOW)
            hidden_out[k] = grad_hidden
            total = total + jnp.sum(grad_hidden.astype(F32), axis=0, keepdims=True)
            grad_normed = back_mult(grad_hidden, fc_ref[...])
            if k == 0:
                own_out[...] = grad_normed
            else:
                sent_out[k - 1][...] = grad_normed.astype(LOW)
        sums_out[...] = total

    shapes = [
        ((4, slots, model), LOW),
        ((slots, model), F32),
        ((4, slots, model), LOW),
        ((4, slots, model), LOW),
        ((4, slots, model), LOW),
        ((4, slots, model), LOW),
        ((slots, model), F32),
        *[((slots, model), LOW)] * 3,
        ((1, model), F32),
        ((model, model), LOW),
        ((model, model), LOW),
    ]
    args = [*got, attended, *proj, *blocks, small]
    return run(kernel, shapes, links.scalars, args, [pltpu.VMEM((model, model), LOW)])


def ff_grads(links, normed, active, hidden, cot, fc2, rows):
    reps, slots, model = normed.shape
    line = links.line
    full = -(-rows // 16) * 16

    def kernel(scalar_ref, *refs):
        normed_ref, active_ref, hidden_ref, cot_ref, fc2_ref = refs[:5]
        mine_out, other_out, branch_own, *branch_sent, scratch = refs[5:]
        c = scalar_ref[1]
        for start, left, right in ((0, normed_ref, hidden_ref), (full, active_ref, cot_ref)):
            total = contract(left[0], right[0])
            for k in range(1, reps):
                total = total + contract(left[k], right[k])
            scratch[...] = total
            for z in range(line):
                for side, out in ((c, mine_out), (1 - c, other_out)):
                    out[z, pl.ds(start, rows), :] = one_of_pair(scratch, z, side, rows)
        for k in range(reps):
            branch = mult(active_ref[k], fc2_ref[...])
            if k == 0:
                branch_own[...] = branch
            else:
                branch_sent[k - 1][...] = branch.astype(LOW)

    shapes = [
        ((line, full + rows, model), LOW),
        ((line, full + rows, model), LOW),
        ((slots, model), F32),
        *[((slots, model), LOW)] * 3,
    ]
    args = [normed, active, hidden, cot, fc2]
    return run(kernel, shapes, links.scalars, args, [pltpu.VMEM((model, model), F32)])


def middle_back(links, own, received, middle, got, small, slots, count):
    def kernel(scalar_ref, own_ref, r1, r2, r3, middle_ref, got_ref, small_ref, *outs):
        grad_out, branch_out, sums_out = outs
        cotangent = own_ref[...] + r1[...].astype(F32) + r2[...].astype(F32) + r3[...].astype(F32)
        unit_rows, scale = unit(middle_ref[...])
        live = live_rows(got_ref, slots, count)
        cot = got_ref[slots : 2 * slots].astype(F32) * live
        grad = cot + norm_back(cotangent, small_ref[1:2], unit_rows, scale)
        grad_out[...] = grad
        branch = grad.astype(LOW)
        branch_out[...] = branch
        sums_out[0:1] = jnp.sum(cotangent * unit_rows, axis=0, keepdims=True)
        sums_out[1:2] = jnp.sum(cotangent, axis=0, keepdims=True)
        sums_out[2:3] = jnp.sum(branch.astype(F32), axis=0, keepdims=True)
        sums_out[3:4] = jnp.sum(cot, axis=0, keepdims=True)

    model = own.shape[1]
    shapes = [((slots, model), F32), ((slots, model), LOW), ((4, model), F32)]
    return run(kernel, shapes, links.scalars, [own, *received, middle, got, small])


def attn_back(links, grads, got, proj, weights, normed, qkv, probs, attended, sums, bias, rows):
    reps, slots, model = normed.shape
    heads = probs.shape[1]
    part = heads * HEAD_DIM
    line = links.line
    full = -(-rows // 16) * 16
    scale = HEAD_DIM**-0.5

    def kernel(scalar_ref, *refs):
        grad_ref, ins = refs[0], refs[1:5]
        p_ref, w_ref, normed_ref, qkv_ref, probs_ref, att_ref, sums_ref, bias_ref = refs[5:13]
        mine_out, other_out, own_out, *sent_out, scratch, grad_qkv = refs[13:]
        c, j = scalar_ref[1], scalar_ref[2]
        proj_rows = p_ref[pl.ds(pl.multiple_of(j * part, part), part), :]
        gain_sum, shift_sum = jnp.zeros((1, model), F32), jnp.zeros((1, model), F32)
        qkv_sum = jnp.zeros((1, 3 * part), F32)
        for k in range(reps):
            grad_att = back_mult(grad_ref[j ^ k], proj_rows).astype(LOW)
            for h in range(heads):
                at = h * HEAD_DIM
                query = qkv_ref[k, :, at : at + HEAD_DIM]
                keys = qkv_ref[k, :, part + at : part + at + HEAD_DIM]
                values = qkv_ref[k, :, 2 * part + at : 2 * part + at + HEAD_DIM]
                prob = probs_ref[k, h]
                cot = grad_att[:, at : at + HEAD_DIM]
                grad_probs = back_mult(cot, values)
                inner = jnp.sum(prob * grad_probs, axis=-1, keepdims=True)
                grad_scores = (prob * (grad_probs - inner)).astype(LOW)
                grad_qkv[k, :, at : at + HEAD_DIM] = (mult(grad_scores, keys) * scale).astype(LOW)
                grad_qkv[k, :, part + at : part + at + HEAD_DIM] = (
                    contract(grad_scores, query) * scale
                ).astype(LOW)
                grad_qkv[k, :, 2 * part + at : 2 * part + at + HEAD_DIM] = contract(
                    prob.astype(LOW), cot
                ).astype(LOW)
            grad_rows = grad_qkv[k]
            qkv_sum = qkv_sum + jnp.sum(grad_rows.astype(F32), axis=0, keepdims=True)
            grad_normed = back_mult(grad_rows, w_ref[:, : 3 * part])
            if k == 0:
                own_out[...] = grad_normed
            else:
                sent_out[k - 1][...] = grad_normed.astype(LOW)
            unit_rows = unit(ins[k][:slots].astype(F32))[0]
            gain_sum = gain_sum + jnp.sum(grad_normed * unit_rows, axis=0, keepdims=True)
            shift_sum = shift_sum + jnp.sum(grad_normed, axis=0, keepdims=True)
        total_qkv = contract(normed_ref[0], grad_qkv[0])
        for k in range(1, reps):
            total_qkv = total_qkv + contract(normed_ref[k], grad_qkv[k])
        scratch[:, : 3 * part] = total_qkv
        for k in range(reps):
            cols = choose(j, [grad_ref[j ^ k, :, p * part : (p + 1) * part] for p in range(4)])
            product = contract(att_ref[k], cols)
            total_proj = product if k == 0 else total_proj + product
        scratch[:, 3 * part :] = total_proj
        spread = lambda v: jnp.concatenate(
            [jnp.where(j == p, v, jnp.zeros_like(v)) for p in range(4)], axis=1
        )
        vectors = jnp.concatenate(
            [
                gain_sum,
                sums_ref[0:1],
                shift_sum,
                sums_ref[1:2],
                spread(qkv_sum[:, :part]),
                spread(qkv_sum[:, 2 * part :]),
                sums_ref[2:4],
                bias_ref[...],
                jnp.zeros((7, model), F32),
            ]
        ).astype(LOW)
        for z in range(line):
            for side, out in ((c, mine_out), (1 - c, other_out)):
                out[z, pl.ds(0, rows), :] = one_of_pair(scratch, z, side, rows)
                out[z, pl.ds(full, 16), :] = vectors

    shapes = [
        ((line, full + 16, model), LOW),
        ((line, full + 16, model), LOW),
        ((slots, model), F32),
        *[((slots, model), LOW)] * 3,
    ]
    args = [grads, *got, proj, weights, normed, qkv, probs, attended, sums, bias]
    scratch = [pltpu.VMEM((model, model), F32), pltpu.VMEM((reps, slots, 3 * part), LOW)]
    return run(kernel, shapes, links.scalars, args, scratch)


def ff_results(links, parts, rows):
    model = parts[0].shape[1]
    shards = links.shards
    full = -(-rows // 16) * 16

    def kernel(scalar_ref, *refs):
        ins, fc_out, fc2_out = refs[:4], refs[4], refs[5]
        j = scalar_ref[2]
        for p in range(4):
            left = choose(j ^ p, [ref[pl.ds(0, rows), :].astype(F32) for ref in ins])
            for s in range(shards):
                at = (s * 4 + p) * rows
                fc_out[:, at : at + rows] = left[:, s * rows : (s + 1) * rows]
            fc2_out[pl.ds(p * rows, rows), :] = choose(
                j ^ p, [ref[pl.ds(full, rows), :].astype(F32) for ref in ins]
            )

    shapes = [((rows, 4 * model), F32), ((4 * rows, model), F32)]
    return run(kernel, shapes, links.scalars, parts)


def attn_results(links, place, parts, rows):
    model = parts[0].shape[1]
    shards = links.shards
    part = model // 4
    full = -(-rows // 16) * 16

    def kernel(scalar_ref, *refs):
        ins, qkv_out, proj_out, gains_out, shifts_out, bias_out = refs[:4], *refs[4:]
        j, s_here = scalar_ref[2], scalar_ref[3]
        for p in range(4):
            block = choose(j ^ p, [ref[pl.ds(0, rows), :].astype(F32) for ref in ins])
            for t in range(3):
                at = t * model + p * part
                qkv_out[:, at : at + part] = block[:, t * part : (t + 1) * part]
            proj_out[:, p * part : (p + 1) * part] = block[:, 3 * part :]
        cut = lambda v: choose(s_here, [v[:, s * rows : (s + 1) * rows] for s in range(shards)])
        low = [cut(ref[pl.ds(full, 16), :].astype(F32)) for ref in ins]
        sums = low[0] + low[1] + low[2] + low[3]
        gains_out[...] = sums[:2]
        shifts_out[...] = sums[2:8]
        for p in range(4):
            bias_out[:, p * rows : (p + 1) * rows] = choose(j ^ p, [v[8:9] for v in low])

    shapes = [
        ((rows, 3 * model), F32),
        ((rows, model), F32),
        ((2, rows), F32),
        ((6, rows), F32),
        ((1, 4 * rows), F32),
    ]
    scalars = jnp.concatenate([links.scalars, place[None].astype(jnp.int32)])
    return run(kernel, shapes, scalars, parts)


def local(tokens, out_grad, lengths, gains, shifts, w_qkv, w_proj, w_fc, bias_fc, w_fc2):
    links = Links()
    line, shards = links.line, links.shards
    z, c, j = links.z, links.c, links.j
    place = lax.axis_index("shard")
    slots, model = tokens.shape
    count = lengths.shape[1]
    rows = w_proj.shape[0]
    quarter = w_fc2.shape[0] // 4
    assert quarter == rows and w_fc.shape[1] == 4 * model
    heads = model // HEAD_DIM // 4
    part = heads * HEAD_DIM
    full_rows = -(-rows // 16) * 16

    args = [tokens, out_grad, lengths, gains, shifts, bias_fc.reshape(1, -1), w_qkv, w_proj]
    attn_block, sent = pack_attn(links, place, args, slots, rows, part, full_rows)
    w_fc, w_fc2 = tie((w_fc, w_fc2), attn_block)
    ff_block = pack_ff(links, w_fc, w_fc2, rows, full_rows)

    attn_mine = line_gather(links, attn_block)
    got = links.rep_gather(sent)
    attn_mine, got, ff_block = lax.optimization_barrier((attn_mine, got, ff_block))
    attn_blocks = with_partners(links, attn_mine)
    ff_mine = line_gather(links, ff_block)

    proj = proj_lanes(links, attn_blocks, rows, part)
    proj = links.rep_gather(proj)
    weights, normed_one, qkv, probs, sent, small_f = attn_forward(
        links, got, attn_blocks, slots, heads, count, rows
    )
    ff_blocks = with_partners(links, tie(ff_mine, sent))
    attended = lax.all_gather(sent, "rep", axis=0)
    (
        attended,
        middle,
        normed_two,
        active,
        grad_hidden,
        cot,
        own,
        sent_x,
        sent_y,
        sent_d,
        bias_sums,
        proj,
        fc2,
    ) = ff_both(links, got, attended, proj, ff_blocks, small_f, slots, count, rows)
    received = [links.rep(v, k) for k, v in ((1, sent_x), (2, sent_y), (3, sent_d))]
    ff_mine, ff_other, branch, *branch_sent = ff_grads(
        links, normed_two, active, grad_hidden, cot, fc2, rows
    )
    ff_theirs = links.core(tie(ff_other, received))
    grad_middle, grad_branch, sums = middle_back(
        links, own, received, middle, got[0], small_f, slots, count
    )
    ff_sent, ff_own = line_sum(links, ff_mine, ff_theirs)
    grad_branch = lax.all_gather(grad_branch, "rep", axis=0)
    ff_sum = line_send(links, ff_sent, ff_own)
    branch_sent = tie(branch_sent, grad_branch)

    attn_mine, attn_other, own, *sent = attn_back(
        links,
        grad_branch,
        got,
        proj,
        weights,
        normed_one,
        qkv,
        probs,
        attended,
        sums,
        bias_sums,
        rows,
    )
    attn_theirs = links.core(tie(attn_other, ff_sum))
    attn_sent, attn_own = line_sum(links, attn_mine, attn_theirs)
    attn_sum = line_send(links, attn_sent, attn_own)

    for k in range(1, 4):
        branch = branch + links.rep(branch_sent[k - 1], k).astype(F32)
        own = own + links.rep(sent[k - 1], k).astype(F32)
    live = (jnp.arange(slots) < jnp.sum(lengths)).astype(F32)[:, None]
    mixed_out = ((middle + branch + small_f[7]) * live).astype(LOW)
    unit_rows, scale = unit(tokens.astype(F32))
    grad_tokens = grad_middle + norm_back(own, small_f[0], unit_rows, scale)

    fc_out, fc2_out = ff_results(links, links.rep_gather(ff_sum.astype(LOW)), rows)
    qkv_out, proj_out, gains_out, shifts_out, bias_out = attn_results(
        links, place, links.rep_gather(attn_sum.astype(LOW)), rows
    )
    return (
        mixed_out,
        grad_tokens,
        gains_out,
        shifts_out,
        qkv_out,
        proj_out,
        fc_out,
        bias_out.reshape(-1),
        fc2_out,
    )


def solution(mesh):
    return jax.shard_map(
        local,
        mesh=mesh,
        in_specs=(
            P(("rep", "shard"), None),
            P(("rep", "shard"), None),
            P(("rep", "shard"), None),
            P(None, "shard"),
            P(None, "shard"),
            P("shard", None),
            P("shard", None),
            P("shard", None),
            P("shard"),
            P("shard", None),
        ),
        out_specs=(
            P(("rep", "shard"), None),
            P(("rep", "shard"), None),
            P(None, "shard"),
            P(None, "shard"),
            P("shard", None),
            P("shard", None),
            P("shard", None),
            P("shard"),
            P("shard", None),
        ),
        check_vma=False,
    )
```

```python
from functools import partial

import jax
import jax.numpy as jnp
from jax import lax
from jax.experimental import pallas as pl
from jax.experimental.pallas import tpu as pltpu
from jax.sharding import PartitionSpec as P

HEAD_DIM = 64
EPS = 1e-05
LOW = jnp.bfloat16
F32 = jnp.float32


def normalize(values, gain_row, shift_row):
    row_mean = jnp.mean(values, axis=-1, keepdims=True)
    centered = values - row_mean
    variance = jnp.mean(centered * centered, axis=-1, keepdims=True)
    return centered * lax.rsqrt(variance + EPS) * gain_row + shift_row


def contract(left_rows, right_rows):
    return lax.dot_general(
        left_rows, right_rows, (((0,), (0,)), ((), ())), preferred_element_type=F32
    )


def back_mult(grad_rows, weight):
    return lax.dot_general(
        grad_rows, weight, (((1,), (1,)), ((), ())), preferred_element_type=F32
    )


def mult(left, right):
    return jnp.dot(left, right, preferred_element_type=F32)


class Links:
    def __init__(self):
        self.shards = lax.axis_size("shard")
        self.line = self.shards // 2
        place = lax.axis_index("shard")
        self.z = place // 2
        self.c = place % 2
        self.j = lax.axis_index("rep")
        self.scalars = jnp.stack([self.z, self.c, self.j, place]).astype(jnp.int32)
        assert lax.axis_size("rep") == 4

    def core(self, v):
        return lax.ppermute(v, "shard", [(i, i ^ 1) for i in range(self.shards)])

    def along(self, v, hop):
        n = self.shards
        return lax.ppermute(v, "shard", [(i, (i + 2 * hop) % n) for i in range(n)])

    def rep(self, v, k):
        return lax.ppermute(v, "rep", [(i, i ^ k) for i in range(4)])

    def rep_gather(self, v):
        return [v] + [self.rep(v, k) for k in range(1, 4)]


def pick(stack, index, axis=0):
    return lax.dynamic_index_in_dim(stack, index, axis, keepdims=False)


def run(kernel, out_shapes, scalars, args, scratch=()):
    return pl.pallas_call(
        kernel,
        out_shape=[jax.ShapeDtypeStruct(shape, dtype) for shape, dtype in out_shapes],
        in_specs=[pl.BlockSpec(memory_space=pltpu.SMEM)]
        + [pl.BlockSpec(memory_space=pltpu.VMEM)] * len(args),
        out_specs=[pl.BlockSpec(memory_space=pltpu.VMEM)] * len(out_shapes),
        scratch_shapes=list(scratch),
        compiler_params=pltpu.CompilerParams(vmem_limit_bytes=56 * 1024 * 1024),
        cost_estimate=pl.CostEstimate(flops=1, bytes_accessed=1, transcendentals=0),
    )(scalars, *args)


def tie(value, *others):
    return lax.optimization_barrier((value, others))[0]


def line_gather(links, block, end=None):
    return [block] + [links.along(block, hop) for hop in range(1, end or links.line)]


def with_partners(links, mine):
    return mine + [links.core(v) for v in mine]


def assemble(scalar_ref, refs, out, start, rows):
    line = len(refs) // 2
    z, c = scalar_ref[0], scalar_ref[1]
    for hop in range(line):
        at = lax.rem(z + line - hop, line)
        for side in range(2):
            to = (2 * at + c) if side == 0 else (2 * at + 1 - c)
            block = refs[side * line + hop][pl.ds(start, rows), :]
            if rows % 16 == 0:
                out[pl.ds(pl.multiple_of(to * rows, 16), rows), :] = block
                continue
            for s in range(2 * line):

                @pl.when(to == s)
                def _(block=block, s=s):
                    out[s * rows : (s + 1) * rows, :] = block


def store_pieces(scalar_ref, scratch, first, outs, start):
    mine, other = outs
    rows = scratch.shape[1]
    line = scratch.shape[0] // 2
    pitch = mine.shape[0] // line
    for s in range(2 * line):
        scratch[s] = first[s * rows : (s + 1) * rows]
    z, c = scalar_ref[0], scalar_ref[1]
    for hop in range(line):
        at = 2 * lax.rem(z + hop, line)
        to = pl.ds(hop * pitch + start, rows)
        mine[to, :] = scratch[at + c].astype(LOW)
        other[to, :] = scratch[at + 1 - c].astype(LOW)


def line_sum(line, mine, theirs):
    rows = mine.shape[0] // line
    both = [
        mine[hop * rows : (hop + 1) * rows].astype(F32)
        + theirs[hop * rows : (hop + 1) * rows].astype(F32)
        for hop in range(line)
    ]
    return [v.astype(LOW) for v in both[1:]], both[0]


def line_send(links, sent, own):
    for hop, value in enumerate(sent, start=1):
        own = own + links.along(value, hop).astype(F32)
    return own


def pad_rows(v, rows):
    return v if v.shape[0] == rows else jnp.pad(v, ((0, rows - v.shape[0]), (0, 0)))


def unit(values):
    row_mean = jnp.mean(values, axis=-1, keepdims=True)
    centered = values - row_mean
    variance = jnp.mean(centered * centered, axis=-1, keepdims=True)
    scale = lax.rsqrt(variance + EPS)
    return centered * scale, scale


def norm_back(cotangent, gain, unit_rows, scale):
    weighted = cotangent * gain
    return scale * (
        weighted
        - jnp.mean(weighted, axis=-1, keepdims=True)
        - unit_rows * jnp.mean(weighted * unit_rows, axis=-1, keepdims=True)
    )


def gelu_pair(x):
    root = 0.7978845608028654
    square = x * x
    bend = jnp.tanh(root * x * (1.0 + 0.044715 * square))
    half = 0.5 * (1.0 + bend)
    slope = half + 0.5 * x * (1.0 - bend * bend) * root * (1.0 + 3 * 0.044715 * square)
    return x * half, slope


def choose(index, options):
    value = options[0]
    for k in range(1, len(options)):
        value = jnp.where(index == k, options[k], value)
    return value


def live_rows(got, slots, count):
    total = jnp.zeros((1, 1), F32)
    for s in range(count):
        total = total + got[slots : slots + 1, s : s + 1].astype(F32)
    place = lax.broadcasted_iota(jnp.int32, (slots, 1), 0).astype(F32)
    return (place < total).astype(F32)


def pack_attn(links, args, rows, part, full):
    gains, shifts, bias, w_qkv, w_proj = args
    model = w_proj.shape[1]

    def kernel(scalar_ref, gain, shift, bias_ref, qkv_ref, p_ref, out):
        j, s_here = scalar_ref[2], scalar_ref[3]
        for t in range(3):
            out[pl.ds(0, rows), t * part : (t + 1) * part] = choose(
                j,
                [
                    qkv_ref[:, t * model + p * part : t * model + (p + 1) * part]
                    for p in range(4)
                ],
            )
        out[pl.ds(0, rows), 3 * part :] = choose(
            j, [p_ref[:, p * part : (p + 1) * part] for p in range(4)]
        )
        bias_row = bias_ref[...].reshape(1, 4 * rows)
        mine = choose(j, [bias_row[:, p * rows : (p + 1) * rows] for p in range(4)])
        small = jnp.concatenate(
            [v.astype(F32) for v in (gain[...], shift[...], mine)] + [jnp.zeros((7, rows), F32)]
        )
        small = jnp.concatenate([small] * links.shards, axis=1)
        lane = lax.broadcasted_iota(jnp.int32, small.shape, 1)
        here = (lane >= s_here * rows) & (lane < (s_here + 1) * rows)
        out[pl.ds(full, 16), :] = jnp.where(here, small, 0.0).astype(LOW)

    return run(kernel, [((full + 16, model), LOW)], links.scalars, args)[0]


def pack_slots(links, tokens, lengths):
    slots, model = tokens.shape
    count = lengths.shape[1]

    def kernel(scalar_ref, tok, len_ref, sent):
        sent[pl.ds(0, slots), :] = tok[...]
        sent[pl.ds(slots, 16), :] = jnp.zeros((16, model), LOW)
        sent[slots : slots + 1, :count] = len_ref[...].astype(F32).astype(LOW)

    shapes = [((slots + 16, model), LOW)]
    return run(kernel, shapes, links.scalars, [tokens, lengths])[0]


def pack_ff(links, w_fc, w_fc2, rows, full):
    model = w_fc2.shape[1]

    def kernel(scalar_ref, fc_ref, fc2_ref, out):
        j = scalar_ref[2]
        for s in range(links.shards):
            out[pl.ds(0, rows), s * rows : (s + 1) * rows] = choose(
                j,
                [fc_ref[:, (4 * s + p) * rows : (4 * s + p + 1) * rows] for p in range(4)],
            )
        out[pl.ds(full, rows), :] = choose(
            j, [fc2_ref[p * rows : (p + 1) * rows, :] for p in range(4)]
        )

    return run(kernel, [((full + rows, model), LOW)], links.scalars, [w_fc, w_fc2])[0]


def proj_lanes(links, blocks, out_grad, rows, part):
    model = blocks[0].shape[1]
    line = links.line

    def kernel(scalar_ref, *refs):
        ins, cot, mine, other, scratch = refs[:-4], *refs[-4:]
        mine[pl.ds(part // 2, cot.shape[0]), :] = cot[...]
        assemble(scalar_ref, [ref.at[:, pl.ds(512, 256)] for ref in ins], scratch, 0, rows)
        c = scalar_ref[1]
        for out, side in ((mine, c), (other, 1 - c)):
            for g in range(4):
                at = pl.ds(pl.multiple_of(g * part + side * (part // 2), 16), part // 2)
                out[pl.ds(0, part // 2), g * part : (g + 1) * part] = scratch[at, 64:]

    shapes = [((part // 2 + out_grad.shape[0], model), LOW), ((part // 2, model), LOW)]
    scratch = [pltpu.VMEM((model, 256), LOW)]
    return run(kernel, shapes, links.scalars, [*blocks, out_grad], scratch)


def attn_forward(links, got, blocks, slots, heads, count, rows):
    model = blocks[0].shape[1]
    part = heads * HEAD_DIM
    full = -(-rows // 16) * 16

    def kernel(scalar_ref, *refs):
        ins, parts = refs[:4], refs[4 : 4 + len(blocks)]
        w_ref, unit_out, qkv_out, probs_out, sent_out, small_out = refs[4 + len(blocks) :]
        j = scalar_ref[2]
        assemble(scalar_ref, parts, w_ref, 0, rows)
        small_sum = jnp.zeros(small_out.shape, F32)
        for ref in parts:
            small_sum = small_sum + ref[pl.ds(full, 16), :].astype(F32)
        small_out[...] = small_sum
        cut = lambda row: choose(
            j, [small_sum[row : row + 1, p * part : (p + 1) * part] for p in range(4)]
        )
        q_bias, v_bias = cut(4), cut(5)
        rows_at = lax.broadcasted_iota(jnp.int32, (slots, slots), 0).astype(F32)
        cols_at = lax.broadcasted_iota(jnp.int32, (slots, slots), 1).astype(F32)
        for k in range(4):
            normed = unit(ins[k][:slots].astype(F32))[0] * small_sum[0:1] + small_sum[2:3]
            unit_out[k * slots : (k + 1) * slots] = normed.astype(LOW)
        qkv = mult(unit_out[...], w_ref[:, : 3 * part])
        qkv_out[:, :part] = (qkv[:, :part] + q_bias).astype(LOW)
        qkv_out[:, part : 2 * part] = qkv[:, part : 2 * part].astype(LOW)
        qkv_out[:, 2 * part :] = (qkv[:, 2 * part :] + v_bias).astype(LOW)
        for k in range(4):
            block = slice(k * slots, (k + 1) * slots)
            end = jnp.zeros((1, 1), F32)
            row_seq, col_seq = jnp.zeros((slots, slots), F32), jnp.zeros((slots, slots), F32)
            for s in range(count):
                end = end + ins[k][slots : slots + 1, s : s + 1].astype(F32)
                row_seq = row_seq + (end <= rows_at).astype(F32)
                col_seq = col_seq + (end <= cols_at).astype(F32)
            allowed = (row_seq == col_seq) & (cols_at <= rows_at)
            for h in range(heads):
                at = h * HEAD_DIM
                query = qkv_out[block, at : at + HEAD_DIM]
                keys = qkv_out[block, part + at : part + at + HEAD_DIM]
                values = qkv_out[block, 2 * part + at : 2 * part + at + HEAD_DIM]
                scores = back_mult(query, keys) * (HEAD_DIM**-0.5)
                scores = jnp.where(allowed, scores, -1000000000.0)
                exponent = jnp.exp(scores - jnp.max(scores, axis=-1, keepdims=True))
                probs = exponent / jnp.sum(exponent, axis=-1, keepdims=True)
                probs_out[k, h] = probs
                attended = mult(probs.astype(LOW), values)
                to = k * part + at
                sent_out[:, to : to + HEAD_DIM] = attended.astype(LOW)

    shapes = [
        ((model, model), LOW),
        ((4 * slots, model), LOW),
        ((4 * slots, 3 * part), LOW),
        ((4, heads, slots, slots), F32),
        ((slots, 4 * part), LOW),
        ((16, model), F32),
    ]
    return run(kernel, shapes, links.scalars, [*got, *blocks])


def ff_both(links, got, attended, proj, blocks, small, slots, count, rows):
    model = blocks[0].shape[1]
    part = model // 4
    full = -(-rows // 16) * 16
    held = 4 + 1 + 8 + len(blocks) + 1

    def kernel(scalar_ref, *refs):
        ins, att, p_parts, parts, small_ref = (
            refs[:4],
            refs[4],
            refs[5:13],
            refs[13 : held - 1],
            refs[held - 1],
        )
        att_out, middle_out, normed_out, active_out, hidden_out, cot_out = refs[held : held + 6]
        own_out, *sent_out = refs[held + 6 : held + 10]
        sums_out, p_ref, fc2_ref, fc_ref = refs[held + 10 :]
        c, j = scalar_ref[1], scalar_ref[2]
        assemble(scalar_ref, parts, fc_ref, 0, rows)
        assemble(scalar_ref, parts, fc2_ref, full, rows)
        for p in range(4):
            for g in range(4):
                for side, half in ((c, p_parts[:4]), (1 - c, p_parts[4:])):
                    at = pl.ds(pl.multiple_of(g * part + side * (part // 2), 16), part // 2)
                    p_ref[at, p * part : (p + 1) * part] = choose(
                        j ^ p, [ref[: part // 2, g * part : (g + 1) * part] for ref in half]
                    )
        total = jnp.zeros((1, model), F32)
        for k in range(4):
            for p in range(4):
                att_out[k * slots : (k + 1) * slots, p * part : (p + 1) * part] = choose(
                    j ^ p, [att[p, :, (k ^ m) * part : ((k ^ m) + 1) * part] for m in range(4)]
                )
        for first in (0, 2):
            both = (first, first + 1)
            block = slice(first * slots, (first + 2) * slots)
            middle = jnp.concatenate([ins[k][:slots].astype(F32) for k in both])
            middle = middle + mult(att_out[block], p_ref[...]) + small_ref[6:7]
            if first == 0:
                middle_out[...] = middle[:slots]
            normed = (unit(middle)[0] * small_ref[1:2] + small_ref[3:4]).astype(LOW)
            normed_out[block] = normed
            hidden = mult(normed, fc_ref[...]) + small_ref[8:9]
            active, slope = gelu_pair(hidden)
            active_out[block] = active.astype(LOW)
            cot = jnp.concatenate(
                [
                    p_parts[k][part // 2 :].astype(F32) * live_rows(ins[k], slots, count)
                    for k in both
                ]
            ).astype(LOW)
            cot_out[block] = cot
            grad_hidden = (back_mult(cot, fc2_ref[...]) * slope).astype(LOW)
            hidden_out[block] = grad_hidden
            total = total + jnp.sum(grad_hidden.astype(F32), axis=0, keepdims=True)
            grad_normed = back_mult(grad_hidden, fc_ref[...])
            for k in both:
                grad_rows = grad_normed[(k - first) * slots : (k - first + 1) * slots]
                if k == 0:
                    own_out[...] = grad_rows
                else:
                    sent_out[k - 1][...] = grad_rows.astype(LOW)
        sums_out[...] = total

    shapes = [
        ((4 * slots, model), LOW),
        ((slots, model), F32),
        ((4 * slots, model), LOW),
        ((4 * slots, model), LOW),
        ((4 * slots, model), LOW),
        ((4 * slots, model), LOW),
        ((slots, model), F32),
        *[((slots, model), LOW)] * 3,
        ((1, model), F32),
        ((model, model), LOW),
        ((model, model), LOW),
    ]
    args = [*got, attended, *proj, *blocks, small]
    return run(kernel, shapes, links.scalars, args, [pltpu.VMEM((model, model), LOW)])


def ff_grads(links, normed, active, hidden, cot, fc2, slots, rows):
    model = normed.shape[1]
    line = links.line
    full = -(-rows // 16) * 16

    def kernel(scalar_ref, *refs):
        normed_ref, active_ref, hidden_ref, cot_ref, fc2_ref = refs[:5]
        pieces = refs[5:7]
        branch_own, *branch_sent, scratch = refs[7:]
        for start, left, right in ((0, normed_ref, hidden_ref), (full, active_ref, cot_ref)):
            store_pieces(scalar_ref, scratch, contract(left[...], right[...]), pieces, start)
        branch = mult(active_ref[...], fc2_ref[...])
        branch_own[...] = branch[:slots]
        for k in range(1, 4):
            branch_sent[k - 1][...] = branch[k * slots : (k + 1) * slots].astype(LOW)

    shapes = [
        *[((line * (full + rows), model), LOW)] * 2,
        ((slots, model), F32),
        *[((slots, model), LOW)] * 3,
    ]
    args = [normed, active, hidden, cot, fc2]
    return run(kernel, shapes, links.scalars, args, [pltpu.VMEM((2 * line, rows, model), F32)])


def middle_back(links, own, received, middle, got, out_grad, small, slots, count):
    def kernel(scalar_ref, own_ref, r1, r2, r3, middle_ref, got_ref, cot_ref, small_ref, *outs):
        grad_out, branch_out, sums_out = outs
        cotangent = own_ref[...] + r1[...].astype(F32) + r2[...].astype(F32) + r3[...].astype(F32)
        unit_rows, scale = unit(middle_ref[...])
        live = live_rows(got_ref, slots, count)
        cot = cot_ref[...].astype(F32) * live
        grad = cot + norm_back(cotangent, small_ref[1:2], unit_rows, scale)
        grad_out[...] = grad
        branch = grad.astype(LOW)
        branch_out[...] = branch
        sums_out[0:1] = jnp.sum(cotangent * unit_rows, axis=0, keepdims=True)
        sums_out[1:2] = jnp.sum(cotangent, axis=0, keepdims=True)
        sums_out[2:3] = jnp.sum(branch.astype(F32), axis=0, keepdims=True)
        sums_out[3:4] = jnp.sum(cot, axis=0, keepdims=True)

    model = own.shape[1]
    shapes = [((slots, model), F32), ((slots, model), LOW), ((4, model), F32)]
    return run(kernel, shapes, links.scalars, [own, *received, middle, got, out_grad, small])


def attn_back(
    links,
    grads,
    got,
    proj,
    weights,
    normed,
    qkv,
    probs,
    attended,
    sums,
    bias,
    slots,
    rows,
):
    model = normed.shape[1]
    heads = probs.shape[1]
    part = heads * HEAD_DIM
    line = links.line
    full = -(-rows // 16) * 16
    scale = HEAD_DIM**-0.5

    def kernel(scalar_ref, *refs):
        grad_ref, ins = refs[0], refs[1:5]
        p_ref, w_ref, normed_ref, qkv_ref, probs_ref, att_ref, sums_ref, bias_ref = refs[5:13]
        pieces = refs[13:15]
        own_out, *sent_out, scratch, grad_qkv, branch, cols = refs[15:]
        j = scalar_ref[2]
        for k in range(4):
            block = slice(k * slots, (k + 1) * slots)
            branch[block] = grad_ref[j ^ k]
            cols[block] = choose(
                j, [grad_ref[j ^ k, :, p * part : (p + 1) * part] for p in range(4)]
            )
        proj_rows = p_ref[pl.ds(pl.multiple_of(j * part, part), part), :]
        grad_att = back_mult(branch[...], proj_rows).astype(LOW)
        for k in range(4):
            block = slice(k * slots, (k + 1) * slots)
            for h in range(heads):
                at = h * HEAD_DIM
                query = qkv_ref[block, at : at + HEAD_DIM]
                keys = qkv_ref[block, part + at : part + at + HEAD_DIM]
                values = qkv_ref[block, 2 * part + at : 2 * part + at + HEAD_DIM]
                prob = probs_ref[k, h]
                cot = grad_att[block, at : at + HEAD_DIM]
                grad_probs = back_mult(cot, values)
                inner = jnp.sum(prob * grad_probs, axis=-1, keepdims=True)
                grad_scores = (prob * (grad_probs - inner)).astype(LOW)
                grad_qkv[block, at : at + HEAD_DIM] = (mult(grad_scores, keys) * scale).astype(LOW)
                grad_qkv[block, part + at : part + at + HEAD_DIM] = (
                    contract(grad_scores, query) * scale
                ).astype(LOW)
                grad_qkv[block, 2 * part + at : 2 * part + at + HEAD_DIM] = contract(
                    prob.astype(LOW), cot
                ).astype(LOW)
        grad_rows = grad_qkv[...]
        qkv_sum = jnp.sum(grad_rows.astype(F32), axis=0, keepdims=True)
        grad_normed = back_mult(grad_rows, w_ref[:, : 3 * part])
        own_out[...] = grad_normed[:slots]
        for k in range(1, 4):
            sent_out[k - 1][...] = grad_normed[k * slots : (k + 1) * slots].astype(LOW)
        gain_sum = jnp.zeros((1, model), F32)
        for k in range(4):
            unit_rows = unit(ins[k][:slots].astype(F32))[0]
            block = slice(k * slots, (k + 1) * slots)
            gain_sum = gain_sum + jnp.sum(grad_normed[block] * unit_rows, axis=0, keepdims=True)
        shift_sum = jnp.sum(grad_normed, axis=0, keepdims=True)
        total = jnp.concatenate(
            [contract(normed_ref[...], grad_rows), contract(att_ref[...], cols[...])], axis=1
        )
        store_pieces(scalar_ref, scratch, total, pieces, 0)
        spread = lambda v: jnp.concatenate(
            [jnp.where(j == p, v, jnp.zeros_like(v)) for p in range(4)], axis=1
        )
        vectors = jnp.concatenate(
            [
                gain_sum,
                sums_ref[0:1],
                shift_sum,
                sums_ref[1:2],
                spread(qkv_sum[:, :part]),
                spread(qkv_sum[:, 2 * part :]),
                sums_ref[2:4],
                bias_ref[...],
                jnp.zeros((7, model), F32),
            ]
        ).astype(LOW)
        for out in pieces:
            for hop in range(line):
                out[pl.ds(hop * (full + 16) + full, 16), :] = vectors

    shapes = [
        *[((line * (full + 16), model), LOW)] * 2,
        ((slots, model), F32),
        *[((slots, model), LOW)] * 3,
    ]
    args = [grads, *got, proj, weights, normed, qkv, probs, attended, sums, bias]
    scratch = [
        pltpu.VMEM((2 * line, rows, model), F32),
        pltpu.VMEM((4 * slots, 3 * part), LOW),
        pltpu.VMEM((4 * slots, model), LOW),
        pltpu.VMEM((4 * slots, part), LOW),
    ]
    return run(kernel, shapes, links.scalars, args, scratch)


def ff_results(links, parts, rows):
    model = parts[0].shape[1]
    shards = links.shards
    full = -(-rows // 16) * 16

    def kernel(scalar_ref, *refs):
        ins, fc_out, fc2_out = refs[:4], refs[4], refs[5]
        j = scalar_ref[2]
        for p in range(4):
            left = choose(j ^ p, [ref[pl.ds(0, rows), :].astype(F32) for ref in ins])
            for s in range(shards):
                at = (s * 4 + p) * rows
                fc_out[:, at : at + rows] = left[:, s * rows : (s + 1) * rows]
            fc2_out[pl.ds(p * rows, rows), :] = choose(
                j ^ p, [ref[pl.ds(full, rows), :].astype(F32) for ref in ins]
            )

    shapes = [((rows, 4 * model), F32), ((4 * rows, model), F32)]
    return run(kernel, shapes, links.scalars, parts)


def attn_results(links, parts, rows):
    model = parts[0].shape[1]
    shards = links.shards
    part = model // 4
    full = -(-rows // 16) * 16

    def kernel(scalar_ref, *refs):
        ins, qkv_out, proj_out, gains_out, shifts_out, bias_out = refs[:4], *refs[4:]
        j, s_here = scalar_ref[2], scalar_ref[3]
        for p in range(4):
            block = choose(j ^ p, [ref[pl.ds(0, rows), :].astype(F32) for ref in ins])
            for t in range(3):
                at = t * model + p * part
                qkv_out[:, at : at + part] = block[:, t * part : (t + 1) * part]
            proj_out[:, p * part : (p + 1) * part] = block[:, 3 * part :]
        cut = lambda v: choose(s_here, [v[:, s * rows : (s + 1) * rows] for s in range(shards)])
        low = [cut(ref[pl.ds(full, 16), :].astype(F32)) for ref in ins]
        sums = low[0] + low[1] + low[2] + low[3]
        gains_out[...] = sums[:2]
        shifts_out[...] = sums[2:8]
        bias = jnp.concatenate([choose(j ^ p, [v[8:9] for v in low]) for p in range(4)], axis=1)
        bias_out[...] = bias.reshape(bias_out.shape)

    shapes = [
        ((rows, 3 * model), F32),
        ((rows, model), F32),
        ((2, rows), F32),
        ((6, rows), F32),
        ((4 * rows,), F32),
    ]
    return run(kernel, shapes, links.scalars, parts)


def local(tokens, out_grad, lengths, gains, shifts, w_qkv, w_proj, w_fc, bias_fc, w_fc2):
    links = Links()
    line, shards = links.line, links.shards
    z, c, j = links.z, links.c, links.j
    slots, model = tokens.shape
    count = lengths.shape[1]
    rows = w_proj.shape[0]
    quarter = w_fc2.shape[0] // 4
    assert quarter == rows and w_fc.shape[1] == 4 * model
    heads = model // HEAD_DIM // 4
    part = heads * HEAD_DIM
    full_rows = -(-rows // 16) * 16

    attn_block = pack_attn(links, [gains, shifts, bias_fc, w_qkv, w_proj], rows, part, full_rows)
    sent = pack_slots(links, tie(tokens, attn_block), lengths)
    w_fc, w_fc2 = tie((w_fc, w_fc2), sent)
    ff_block = pack_ff(links, w_fc, w_fc2, rows, full_rows)

    attn_mine = line_gather(links, attn_block)
    got = links.rep_gather(sent)
    attn_mine, got, ff_block = lax.optimization_barrier((attn_mine, got, ff_block))
    attn_blocks = with_partners(links, attn_mine)
    ff_mine = line_gather(links, ff_block, links.line - 1)

    proj_mine, proj_other = proj_lanes(links, attn_blocks, out_grad, rows, part)
    proj = links.rep_gather(proj_mine)
    attn_blocks = tie(attn_blocks, proj_mine)
    weights, normed_one, qkv, probs, sent, small_f = attn_forward(
        links, got, attn_blocks, slots, heads, count, rows
    )
    ff_mine.append(links.along(tie(ff_block, sent), line - 1))
    attended = lax.all_gather(sent, "rep", axis=0)
    proj, ff_mine = tie((proj, ff_mine), attended)
    proj = proj + [proj_other] + [links.core(v) for v in proj[1:]]
    ff_blocks = with_partners(links, ff_mine)
    (
        attended,
        middle,
        normed_two,
        active,
        grad_hidden,
        cot,
        own,
        sent_x,
        sent_y,
        sent_d,
        bias_sums,
        proj,
        fc2,
    ) = ff_both(links, got, attended, proj, ff_blocks, small_f, slots, count, rows)
    received = [links.rep(v, k) for k, v in ((1, sent_x), (2, sent_y), (3, sent_d))]
    ff_mine, ff_other, branch, sent_x, sent_y, sent_d = ff_grads(
        links, normed_two, active, grad_hidden, cot, fc2, slots, rows
    )
    branch_sent = [sent_x, sent_y, sent_d]
    ff_other = tie(ff_other, received)
    ff_theirs = links.core(ff_other)
    ff_sent, ff_own = line_sum(line, ff_mine, ff_theirs)
    grad_middle, grad_branch, sums = middle_back(
        links, own, received, middle, got[0], out_grad, small_f, slots, count
    )
    grad_branch = lax.all_gather(grad_branch, "rep", axis=0)
    branch_got = [links.rep(v, k) for k, v in enumerate(branch_sent, start=1)]
    grad_branch = tie(grad_branch, branch_got)
    ff_sum = line_send(links, ff_sent, ff_own)

    attn_mine, attn_other, own, sent_x, sent_y, sent_d = attn_back(
        links,
        grad_branch,
        got,
        proj,
        weights,
        normed_one,
        qkv,
        probs,
        attended,
        sums,
        bias_sums,
        slots,
        rows,
    )
    attn_other = tie(attn_other, ff_sum)
    attn_theirs = links.core(attn_other)
    attn_sent, attn_own = line_sum(line, attn_mine, attn_theirs)
    attn_sent = tie(attn_sent, ff_sum)
    attn_sum = line_send(links, attn_sent, attn_own)

    own_sent = [sent_x, sent_y, sent_d]
    own_got = []
    for k in range(1, 4):
        own_got.append(links.rep(own_sent[k - 1], k))
        own = own + own_got[-1].astype(F32)
        branch = branch + branch_got[k - 1].astype(F32)
    live = (jnp.arange(slots) < jnp.sum(lengths)).astype(F32)[:, None]
    mixed_out = ((middle + branch + small_f[7]) * live).astype(LOW)
    unit_rows, scale = unit(tokens.astype(F32))
    grad_tokens = grad_middle + norm_back(own, small_f[0], unit_rows, scale)

    fc_out, fc2_out = ff_results(links, links.rep_gather(tie(ff_sum.astype(LOW), own_got)), rows)
    qkv_out, proj_out, gains_out, shifts_out, bias_out = attn_results(
        links, links.rep_gather(attn_sum.astype(LOW)), rows
    )
    return (
        mixed_out,
        grad_tokens,
        gains_out,
        shifts_out,
        qkv_out,
        proj_out,
        fc_out,
        bias_out,
        fc2_out,
    )


def solution(mesh):
    return jax.shard_map(
        local,
        mesh=mesh,
        in_specs=(
            P(("rep", "shard"), None),
            P(("rep", "shard"), None),
            P(("rep", "shard"), None),
            P(None, "shard"),
            P(None, "shard"),
            P("shard", None),
            P("shard", None),
            P("shard", None),
            P("shard"),
            P("shard", None),
        ),
        out_specs=(
            P(("rep", "shard"), None),
            P(("rep", "shard"), None),
            P(None, "shard"),
            P(None, "shard"),
            P("shard", None),
            P("shard", None),
            P("shard", None),
            P("shard"),
            P("shard", None),
        ),
        check_vma=False,
    )
```

```python
from functools import partial

import jax
import jax.numpy as jnp
from jax import lax
from jax.experimental import pallas as pl
from jax.experimental.pallas import tpu as pltpu
from jax.sharding import PartitionSpec as P

HEAD_DIM = 64
EPS = 1e-05
LOW = jnp.bfloat16
F32 = jnp.float32


def normalize(values, gain_row, shift_row):
    row_mean = jnp.mean(values, axis=-1, keepdims=True)
    centered = values - row_mean
    variance = jnp.mean(centered * centered, axis=-1, keepdims=True)
    return centered * lax.rsqrt(variance + EPS) * gain_row + shift_row


def contract(left_rows, right_rows):
    return lax.dot_general(
        left_rows, right_rows, (((0,), (0,)), ((), ())), preferred_element_type=F32
    )


def back_mult(grad_rows, weight):
    return lax.dot_general(
        grad_rows, weight, (((1,), (1,)), ((), ())), preferred_element_type=F32
    )


def mult(left, right):
    return jnp.dot(left, right, preferred_element_type=F32)


class Links:
    def __init__(self):
        self.shards = lax.axis_size("shard")
        self.line = self.shards // 2
        place = lax.axis_index("shard")
        self.z = place // 2
        self.c = place % 2
        self.j = lax.axis_index("rep")
        self.scalars = jnp.stack([self.z, self.c, self.j, place]).astype(jnp.int32)
        assert lax.axis_size("rep") == 4

    def core(self, v):
        return lax.ppermute(v, "shard", [(i, i ^ 1) for i in range(self.shards)])

    def along(self, v, hop):
        n = self.shards
        return lax.ppermute(v, "shard", [(i, (i + 2 * hop) % n) for i in range(n)])

    def rep(self, v, k):
        return lax.ppermute(v, "rep", [(i, i ^ k) for i in range(4)])

    def rep_gather(self, v):
        return [v] + [self.rep(v, k) for k in range(1, 4)]


def pick(stack, index, axis=0):
    return lax.dynamic_index_in_dim(stack, index, axis, keepdims=False)


def run(kernel, out_shapes, scalars, args, scratch=()):
    return pl.pallas_call(
        kernel,
        out_shape=[jax.ShapeDtypeStruct(shape, dtype) for shape, dtype in out_shapes],
        in_specs=[pl.BlockSpec(memory_space=pltpu.SMEM)]
        + [pl.BlockSpec(memory_space=pltpu.VMEM)] * len(args),
        out_specs=[pl.BlockSpec(memory_space=pltpu.VMEM)] * len(out_shapes),
        scratch_shapes=list(scratch),
        compiler_params=pltpu.CompilerParams(vmem_limit_bytes=56 * 1024 * 1024),
        cost_estimate=pl.CostEstimate(flops=1, bytes_accessed=1, transcendentals=0),
    )(scalars, *args)


def tie(value, *others):
    return lax.optimization_barrier((value, others))[0]


def line_gather(links, block, end=None):
    return [block] + [links.along(block, hop) for hop in range(1, end or links.line)]


def with_partners(links, mine):
    return mine + [links.core(v) for v in mine]


def assemble(scalar_ref, refs, out, start, rows):
    line = len(refs) // 2
    z, c = scalar_ref[0], scalar_ref[1]
    for hop in range(line):
        at = lax.rem(z + line - hop, line)
        for side in range(2):
            to = (2 * at + c) if side == 0 else (2 * at + 1 - c)
            block = refs[side * line + hop][pl.ds(start, rows), :]
            if rows % 16 == 0:
                out[pl.ds(pl.multiple_of(to * rows, 16), rows), :] = block
                continue
            for s in range(2 * line):

                @pl.when(to == s)
                def _(block=block, s=s):
                    out[s * rows : (s + 1) * rows, :] = block


def store_pieces(scalar_ref, scratch, first, outs, start):
    mine, other = outs
    rows = scratch.shape[1]
    line = scratch.shape[0] // 2
    pitch = mine.shape[0] // line
    for s in range(2 * line):
        scratch[s] = first[s * rows : (s + 1) * rows]
    z, c = scalar_ref[0], scalar_ref[1]
    for hop in range(line):
        at = 2 * lax.rem(z + hop, line)
        to = pl.ds(hop * pitch + start, rows)
        mine[to, :] = scratch[at + c].astype(LOW)
        other[to, :] = scratch[at + 1 - c].astype(LOW)


def line_sum(line, mine, theirs):
    rows = mine.shape[0] // line
    both = [
        mine[hop * rows : (hop + 1) * rows].astype(F32)
        + theirs[hop * rows : (hop + 1) * rows].astype(F32)
        for hop in range(line)
    ]
    return [v.astype(LOW) for v in both[1:]], both[0]


def line_send(links, sent, own):
    for hop, value in enumerate(sent, start=1):
        own = own + links.along(value, hop).astype(F32)
    return own


def pad_rows(v, rows):
    return v if v.shape[0] == rows else jnp.pad(v, ((0, rows - v.shape[0]), (0, 0)))


def unit(values):
    row_mean = jnp.mean(values, axis=-1, keepdims=True)
    centered = values - row_mean
    variance = jnp.mean(centered * centered, axis=-1, keepdims=True)
    scale = lax.rsqrt(variance + EPS)
    return centered * scale, scale


def norm_back(cotangent, gain, unit_rows, scale):
    weighted = cotangent * gain
    return scale * (
        weighted
        - jnp.mean(weighted, axis=-1, keepdims=True)
        - unit_rows * jnp.mean(weighted * unit_rows, axis=-1, keepdims=True)
    )


def gelu_pair(x):
    root = 0.7978845608028654
    square = x * x
    bend = jnp.tanh(root * x * (1.0 + 0.044715 * square))
    half = 0.5 * (1.0 + bend)
    slope = half + 0.5 * x * (1.0 - bend * bend) * root * (1.0 + 3 * 0.044715 * square)
    return x * half, slope


def choose(index, options):
    value = options[0]
    for k in range(1, len(options)):
        value = jnp.where(index == k, options[k], value)
    return value


def live_rows(got, slots, count):
    total = jnp.zeros((1, 1), F32)
    for s in range(count):
        total = total + got[slots : slots + 1, s : s + 1].astype(F32)
    place = lax.broadcasted_iota(jnp.int32, (slots, 1), 0).astype(F32)
    return (place < total).astype(F32)


def pack_attn(links, args, rows, part, full):
    gains, shifts, bias, w_qkv, w_proj = args
    model = w_proj.shape[1]

    def kernel(scalar_ref, gain, shift, bias_ref, qkv_ref, p_ref, out):
        j, s_here = scalar_ref[2], scalar_ref[3]
        for t in range(3):
            out[pl.ds(0, rows), t * part : (t + 1) * part] = choose(
                j,
                [
                    qkv_ref[:, t * model + p * part : t * model + (p + 1) * part]
                    for p in range(4)
                ],
            )
        out[pl.ds(0, rows), 3 * part :] = choose(
            j, [p_ref[:, p * part : (p + 1) * part] for p in range(4)]
        )
        bias_row = bias_ref[...].reshape(1, 4 * rows)
        mine = choose(j, [bias_row[:, p * rows : (p + 1) * rows] for p in range(4)])
        small = jnp.concatenate(
            [v.astype(F32) for v in (gain[...], shift[...], mine)] + [jnp.zeros((7, rows), F32)]
        )
        small = jnp.concatenate([small] * links.shards, axis=1)
        lane = lax.broadcasted_iota(jnp.int32, small.shape, 1)
        here = (lane >= s_here * rows) & (lane < (s_here + 1) * rows)
        out[pl.ds(full, 16), :] = jnp.where(here, small, 0.0).astype(LOW)

    return run(kernel, [((full + 16, model), LOW)], links.scalars, args)[0]


def pack_slots(links, tokens, lengths):
    slots, model = tokens.shape
    count = lengths.shape[1]

    def kernel(scalar_ref, tok, len_ref, sent):
        sent[pl.ds(0, slots), :] = tok[...]
        sent[pl.ds(slots, 16), :] = jnp.zeros((16, model), LOW)
        sent[slots : slots + 1, :count] = len_ref[...].astype(F32).astype(LOW)

    shapes = [((slots + 16, model), LOW)]
    return run(kernel, shapes, links.scalars, [tokens, lengths])[0]


def pack_ff(links, w_fc, w_fc2, rows, full):
    model = w_fc2.shape[1]

    def kernel(scalar_ref, fc_ref, fc2_ref, out):
        j = scalar_ref[2]
        for s in range(links.shards):
            out[pl.ds(0, rows), s * rows : (s + 1) * rows] = choose(
                j,
                [fc_ref[:, (4 * s + p) * rows : (4 * s + p + 1) * rows] for p in range(4)],
            )
        out[pl.ds(full, rows), :] = choose(
            j, [fc2_ref[p * rows : (p + 1) * rows, :] for p in range(4)]
        )

    return run(kernel, [((full + rows, model), LOW)], links.scalars, [w_fc, w_fc2])[0]


def proj_lanes(links, blocks, out_grad, rows, part):
    model = blocks[0].shape[1]
    line = links.line

    def kernel(scalar_ref, *refs):
        ins, cot, mine, other, scratch = refs[:-4], *refs[-4:]
        mine[pl.ds(part // 2, cot.shape[0]), :] = cot[...]
        assemble(scalar_ref, [ref.at[:, pl.ds(512, 256)] for ref in ins], scratch, 0, rows)
        c = scalar_ref[1]
        for out, side in ((mine, c), (other, 1 - c)):
            for g in range(4):
                at = pl.ds(pl.multiple_of(g * part + side * (part // 2), 16), part // 2)
                out[pl.ds(0, part // 2), g * part : (g + 1) * part] = scratch[at, 64:]

    shapes = [((part // 2 + out_grad.shape[0], model), LOW), ((part // 2, model), LOW)]
    scratch = [pltpu.VMEM((model, 256), LOW)]
    return run(kernel, shapes, links.scalars, [*blocks, out_grad], scratch)


def attn_forward(links, got, blocks, slots, heads, count, rows):
    model = blocks[0].shape[1]
    part = heads * HEAD_DIM
    full = -(-rows // 16) * 16

    def kernel(scalar_ref, *refs):
        ins, parts = refs[:4], refs[4 : 4 + len(blocks)]
        w_ref, unit_out, qkv_out, probs_out, sent_out, small_out = refs[4 + len(blocks) :]
        j = scalar_ref[2]
        assemble(scalar_ref, parts, w_ref, 0, rows)
        small_sum = jnp.zeros(small_out.shape, F32)
        for ref in parts:
            small_sum = small_sum + ref[pl.ds(full, 16), :].astype(F32)
        small_out[...] = small_sum
        cut = lambda row: choose(
            j, [small_sum[row : row + 1, p * part : (p + 1) * part] for p in range(4)]
        )
        q_bias, v_bias = cut(4), cut(5)
        rows_at = lax.broadcasted_iota(jnp.int32, (slots, slots), 0).astype(F32)
        cols_at = lax.broadcasted_iota(jnp.int32, (slots, slots), 1).astype(F32)
        for k in range(4):
            normed = unit(ins[k][:slots].astype(F32))[0] * small_sum[0:1] + small_sum[2:3]
            unit_out[k * slots : (k + 1) * slots] = normed.astype(LOW)
        qkv = mult(unit_out[...], w_ref[:, : 3 * part])
        qkv_out[:, :part] = (qkv[:, :part] + q_bias).astype(LOW)
        qkv_out[:, part : 2 * part] = qkv[:, part : 2 * part].astype(LOW)
        qkv_out[:, 2 * part :] = (qkv[:, 2 * part :] + v_bias).astype(LOW)
        for k in range(4):
            block = slice(k * slots, (k + 1) * slots)
            end = jnp.zeros((1, 1), F32)
            row_seq, col_seq = jnp.zeros((slots, slots), F32), jnp.zeros((slots, slots), F32)
            for s in range(count):
                end = end + ins[k][slots : slots + 1, s : s + 1].astype(F32)
                row_seq = row_seq + (end <= rows_at).astype(F32)
                col_seq = col_seq + (end <= cols_at).astype(F32)
            allowed = (row_seq == col_seq) & (cols_at <= rows_at)
            for h in range(heads):
                at = h * HEAD_DIM
                query = qkv_out[block, at : at + HEAD_DIM]
                keys = qkv_out[block, part + at : part + at + HEAD_DIM]
                values = qkv_out[block, 2 * part + at : 2 * part + at + HEAD_DIM]
                scores = back_mult(query, keys) * (HEAD_DIM**-0.5)
                scores = jnp.where(allowed, scores, -1000000000.0)
                exponent = jnp.exp(scores - jnp.max(scores, axis=-1, keepdims=True))
                probs = exponent / jnp.sum(exponent, axis=-1, keepdims=True)
                probs_out[k, h] = probs
                attended = mult(probs.astype(LOW), values)
                to = k * part + at
                sent_out[:, to : to + HEAD_DIM] = attended.astype(LOW)

    shapes = [
        ((model, model), LOW),
        ((4 * slots, model), LOW),
        ((4 * slots, 3 * part), LOW),
        ((4, heads, slots, slots), F32),
        ((slots, 4 * part), LOW),
        ((16, model), F32),
    ]
    return run(kernel, shapes, links.scalars, [*got, *blocks])


def ff_both(links, got, attended, proj, blocks, small, slots, count, rows):
    model = blocks[0].shape[1]
    part = model // 4
    full = -(-rows // 16) * 16
    held = 4 + 1 + 8 + len(blocks) + 1

    def kernel(scalar_ref, *refs):
        ins, att, p_parts, parts, small_ref = (
            refs[:4],
            refs[4],
            refs[5:13],
            refs[13 : held - 1],
            refs[held - 1],
        )
        att_out, middle_out, normed_out, active_out, hidden_out, cot_out = refs[held : held + 6]
        own_out, *sent_out = refs[held + 6 : held + 10]
        sums_out, p_ref, fc2_ref, fc_ref = refs[held + 10 :]
        c, j = scalar_ref[1], scalar_ref[2]
        assemble(scalar_ref, parts, fc_ref, 0, rows)
        assemble(scalar_ref, parts, fc2_ref, full, rows)
        for p in range(4):
            for g in range(4):
                for side, half in ((c, p_parts[:4]), (1 - c, p_parts[4:])):
                    at = pl.ds(pl.multiple_of(g * part + side * (part // 2), 16), part // 2)
                    p_ref[at, p * part : (p + 1) * part] = choose(
                        j ^ p, [ref[: part // 2, g * part : (g + 1) * part] for ref in half]
                    )
        total = jnp.zeros((1, model), F32)
        for k in range(4):
            for p in range(4):
                att_out[k * slots : (k + 1) * slots, p * part : (p + 1) * part] = choose(
                    j ^ p, [att[p, :, (k ^ m) * part : ((k ^ m) + 1) * part] for m in range(4)]
                )
        for first in (0, 2):
            both = (first, first + 1)
            block = slice(first * slots, (first + 2) * slots)
            middle = jnp.concatenate([ins[k][:slots].astype(F32) for k in both])
            middle = middle + mult(att_out[block], p_ref[...]) + small_ref[6:7]
            if first == 0:
                middle_out[...] = middle[:slots]
            normed = (unit(middle)[0] * small_ref[1:2] + small_ref[3:4]).astype(LOW)
            normed_out[block] = normed
            hidden = mult(normed, fc_ref[...]) + small_ref[8:9]
            active, slope = gelu_pair(hidden)
            active_out[block] = active.astype(LOW)
            cot = jnp.concatenate(
                [
                    p_parts[k][part // 2 :].astype(F32) * live_rows(ins[k], slots, count)
                    for k in both
                ]
            ).astype(LOW)
            cot_out[block] = cot
            grad_hidden = (back_mult(cot, fc2_ref[...]) * slope).astype(LOW)
            hidden_out[block] = grad_hidden
            total = total + jnp.sum(grad_hidden.astype(F32), axis=0, keepdims=True)
            grad_normed = back_mult(grad_hidden, fc_ref[...])
            for k in both:
                grad_rows = grad_normed[(k - first) * slots : (k - first + 1) * slots]
                if k == 0:
                    own_out[...] = grad_rows
                else:
                    sent_out[k - 1][...] = grad_rows.astype(LOW)
        sums_out[...] = total

    shapes = [
        ((4 * slots, model), LOW),
        ((slots, model), F32),
        ((4 * slots, model), LOW),
        ((4 * slots, model), LOW),
        ((4 * slots, model), LOW),
        ((4 * slots, model), LOW),
        ((slots, model), F32),
        *[((slots, model), LOW)] * 3,
        ((1, model), F32),
        ((model, model), LOW),
        ((model, model), LOW),
    ]
    args = [*got, attended, *proj, *blocks, small]
    return run(kernel, shapes, links.scalars, args, [pltpu.VMEM((model, model), LOW)])


def ff_grads(links, normed, active, hidden, cot, fc2, slots, rows):
    model = normed.shape[1]
    line = links.line
    full = -(-rows // 16) * 16

    def kernel(scalar_ref, *refs):
        normed_ref, active_ref, hidden_ref, cot_ref, fc2_ref = refs[:5]
        pieces = refs[5:7]
        branch_own, *branch_sent, scratch = refs[7:]
        for start, left, right in ((0, normed_ref, hidden_ref), (full, active_ref, cot_ref)):
            store_pieces(scalar_ref, scratch, contract(left[...], right[...]), pieces, start)
        branch = mult(active_ref[...], fc2_ref[...])
        branch_own[...] = branch[:slots]
        for k in range(1, 4):
            branch_sent[k - 1][...] = branch[k * slots : (k + 1) * slots].astype(LOW)

    shapes = [
        *[((line * (full + rows), model), LOW)] * 2,
        ((slots, model), F32),
        *[((slots, model), LOW)] * 3,
    ]
    args = [normed, active, hidden, cot, fc2]
    return run(kernel, shapes, links.scalars, args, [pltpu.VMEM((2 * line, rows, model), F32)])


def middle_back(links, own, received, middle, got, out_grad, small, slots, count):
    def kernel(scalar_ref, own_ref, r1, r2, r3, middle_ref, got_ref, cot_ref, small_ref, *outs):
        grad_out, branch_out, sums_out = outs
        cotangent = own_ref[...] + r1[...].astype(F32) + r2[...].astype(F32) + r3[...].astype(F32)
        unit_rows, scale = unit(middle_ref[...])
        live = live_rows(got_ref, slots, count)
        cot = cot_ref[...].astype(F32) * live
        grad = cot + norm_back(cotangent, small_ref[1:2], unit_rows, scale)
        grad_out[...] = grad
        branch = grad.astype(LOW)
        branch_out[...] = branch
        sums_out[0:1] = jnp.sum(cotangent * unit_rows, axis=0, keepdims=True)
        sums_out[1:2] = jnp.sum(cotangent, axis=0, keepdims=True)
        sums_out[2:3] = jnp.sum(branch.astype(F32), axis=0, keepdims=True)
        sums_out[3:4] = jnp.sum(cot, axis=0, keepdims=True)

    model = own.shape[1]
    shapes = [((slots, model), F32), ((slots, model), LOW), ((4, model), F32)]
    return run(kernel, shapes, links.scalars, [own, *received, middle, got, out_grad, small])


def attn_back(
    links,
    grads,
    got,
    proj,
    weights,
    normed,
    qkv,
    probs,
    attended,
    sums,
    bias,
    slots,
    rows,
):
    model = normed.shape[1]
    heads = probs.shape[1]
    part = heads * HEAD_DIM
    line = links.line
    full = -(-rows // 16) * 16
    scale = HEAD_DIM**-0.5

    def kernel(scalar_ref, *refs):
        grad_ref, ins = refs[0], refs[1:5]
        p_ref, w_ref, normed_ref, qkv_ref, probs_ref, att_ref, sums_ref, bias_ref = refs[5:13]
        pieces = refs[13:15]
        own_out, *sent_out, scratch, grad_qkv, branch, cols = refs[15:]
        j = scalar_ref[2]
        for k in range(4):
            block = slice(k * slots, (k + 1) * slots)
            branch[block] = grad_ref[j ^ k]
            cols[block] = choose(
                j, [grad_ref[j ^ k, :, p * part : (p + 1) * part] for p in range(4)]
            )
        proj_rows = p_ref[pl.ds(pl.multiple_of(j * part, part), part), :]
        grad_att = back_mult(branch[...], proj_rows).astype(LOW)
        for k in range(4):
            block = slice(k * slots, (k + 1) * slots)
            for h in range(heads):
                at = h * HEAD_DIM
                query = qkv_ref[block, at : at + HEAD_DIM]
                keys = qkv_ref[block, part + at : part + at + HEAD_DIM]
                values = qkv_ref[block, 2 * part + at : 2 * part + at + HEAD_DIM]
                prob = probs_ref[k, h]
                cot = grad_att[block, at : at + HEAD_DIM]
                grad_probs = back_mult(cot, values)
                inner = jnp.sum(prob * grad_probs, axis=-1, keepdims=True)
                grad_scores = (prob * (grad_probs - inner)).astype(LOW)
                grad_qkv[block, at : at + HEAD_DIM] = (mult(grad_scores, keys) * scale).astype(LOW)
                grad_qkv[block, part + at : part + at + HEAD_DIM] = (
                    contract(grad_scores, query) * scale
                ).astype(LOW)
                grad_qkv[block, 2 * part + at : 2 * part + at + HEAD_DIM] = contract(
                    prob.astype(LOW), cot
                ).astype(LOW)
        grad_rows = grad_qkv[...]
        qkv_sum = jnp.sum(grad_rows.astype(F32), axis=0, keepdims=True)
        grad_normed = back_mult(grad_rows, w_ref[:, : 3 * part])
        own_out[...] = grad_normed[:slots]
        for k in range(1, 4):
            sent_out[k - 1][...] = grad_normed[k * slots : (k + 1) * slots].astype(LOW)
        gain_sum = jnp.zeros((1, model), F32)
        for k in range(4):
            unit_rows = unit(ins[k][:slots].astype(F32))[0]
            block = slice(k * slots, (k + 1) * slots)
            gain_sum = gain_sum + jnp.sum(grad_normed[block] * unit_rows, axis=0, keepdims=True)
        shift_sum = jnp.sum(grad_normed, axis=0, keepdims=True)
        total = jnp.concatenate(
            [contract(normed_ref[...], grad_rows), contract(att_ref[...], cols[...])], axis=1
        )
        store_pieces(scalar_ref, scratch, total, pieces, 0)
        spread = lambda v: jnp.concatenate(
            [jnp.where(j == p, v, jnp.zeros_like(v)) for p in range(4)], axis=1
        )
        vectors = jnp.concatenate(
            [
                gain_sum,
                sums_ref[0:1],
                shift_sum,
                sums_ref[1:2],
                spread(qkv_sum[:, :part]),
                spread(qkv_sum[:, 2 * part :]),
                sums_ref[2:4],
                bias_ref[...],
                jnp.zeros((7, model), F32),
            ]
        ).astype(LOW)
        for out in pieces:
            for hop in range(line):
                out[pl.ds(hop * (full + 16) + full, 16), :] = vectors

    shapes = [
        *[((line * (full + 16), model), LOW)] * 2,
        ((slots, model), F32),
        *[((slots, model), LOW)] * 3,
    ]
    args = [grads, *got, proj, weights, normed, qkv, probs, attended, sums, bias]
    scratch = [
        pltpu.VMEM((2 * line, rows, model), F32),
        pltpu.VMEM((4 * slots, 3 * part), LOW),
        pltpu.VMEM((4 * slots, model), LOW),
        pltpu.VMEM((4 * slots, part), LOW),
    ]
    return run(kernel, shapes, links.scalars, args, scratch)


def ff_results(links, parts, rows):
    model = parts[0].shape[1]
    shards = links.shards
    full = -(-rows // 16) * 16

    def kernel(scalar_ref, *refs):
        ins, fc_out, fc2_out = refs[:4], refs[4], refs[5]
        j = scalar_ref[2]
        for p in range(4):
            left = choose(j ^ p, [ref[pl.ds(0, rows), :] for ref in ins]).astype(F32)
            for s in range(shards):
                at = (s * 4 + p) * rows
                fc_out[:, at : at + rows] = left[:, s * rows : (s + 1) * rows]
            fc2_out[pl.ds(p * rows, rows), :] = choose(
                j ^ p, [ref[pl.ds(full, rows), :] for ref in ins]
            ).astype(F32)

    shapes = [((rows, 4 * model), F32), ((4 * rows, model), F32)]
    return run(kernel, shapes, links.scalars, parts)


def attn_results(links, got, rows):
    model = got.shape[2]
    shards = links.shards
    part = model // 4
    full = -(-rows // 16) * 16

    def kernel(scalar_ref, *refs):
        got_ref, qkv_out, proj_out, gains_out, shifts_out, bias_out = refs
        s_here = scalar_ref[3]
        for p in range(4):
            block = got_ref[p, pl.ds(0, rows), :].astype(F32)
            for t in range(3):
                at = t * model + p * part
                qkv_out[:, at : at + part] = block[:, t * part : (t + 1) * part]
            proj_out[:, p * part : (p + 1) * part] = block[:, 3 * part :]
        cut = lambda v: choose(s_here, [v[:, s * rows : (s + 1) * rows] for s in range(shards)])
        low = [cut(got_ref[p, pl.ds(full, 16), :].astype(F32)) for p in range(4)]
        sums = low[0] + low[1] + low[2] + low[3]
        gains_out[...] = sums[:2]
        shifts_out[...] = sums[2:8]
        bias = jnp.concatenate([v[8:9] for v in low], axis=1)
        bias_out[...] = bias.reshape(bias_out.shape)

    shapes = [
        ((rows, 3 * model), F32),
        ((rows, model), F32),
        ((2, rows), F32),
        ((6, rows), F32),
        ((4 * rows,), F32),
    ]
    return run(kernel, shapes, links.scalars, [got])


def local(tokens, out_grad, lengths, gains, shifts, w_qkv, w_proj, w_fc, bias_fc, w_fc2):
    links = Links()
    line, shards = links.line, links.shards
    z, c, j = links.z, links.c, links.j
    slots, model = tokens.shape
    count = lengths.shape[1]
    rows = w_proj.shape[0]
    quarter = w_fc2.shape[0] // 4
    assert quarter == rows and w_fc.shape[1] == 4 * model
    heads = model // HEAD_DIM // 4
    part = heads * HEAD_DIM
    full_rows = -(-rows // 16) * 16

    attn_block = pack_attn(links, [gains, shifts, bias_fc, w_qkv, w_proj], rows, part, full_rows)
    sent = pack_slots(links, tie(tokens, attn_block), lengths)
    w_fc, w_fc2 = tie((w_fc, w_fc2), sent)
    ff_block = pack_ff(links, w_fc, w_fc2, rows, full_rows)

    attn_mine = line_gather(links, attn_block)
    got = links.rep_gather(sent)
    attn_mine, got, ff_block = lax.optimization_barrier((attn_mine, got, ff_block))
    attn_blocks = with_partners(links, attn_mine)
    ff_mine = line_gather(links, ff_block, links.line - 1)

    proj_mine, proj_other = proj_lanes(links, attn_blocks, out_grad, rows, part)
    proj = links.rep_gather(proj_mine)
    attn_blocks = tie(attn_blocks, proj_mine)
    weights, normed_one, qkv, probs, sent, small_f = attn_forward(
        links, got, attn_blocks, slots, heads, count, rows
    )
    ff_mine.append(links.along(tie(ff_block, sent), line - 1))
    attended = lax.all_gather(sent, "rep", axis=0)
    proj, ff_mine = tie((proj, ff_mine), attended)
    proj = proj + [proj_other] + [links.core(v) for v in proj[1:]]
    ff_blocks = with_partners(links, ff_mine)
    (
        attended,
        middle,
        normed_two,
        active,
        grad_hidden,
        cot,
        own,
        sent_x,
        sent_y,
        sent_d,
        bias_sums,
        proj,
        fc2,
    ) = ff_both(links, got, attended, proj, ff_blocks, small_f, slots, count, rows)
    received = [links.rep(v, k) for k, v in ((1, sent_x), (2, sent_y), (3, sent_d))]
    ff_mine, ff_other, branch, sent_x, sent_y, sent_d = ff_grads(
        links, normed_two, active, grad_hidden, cot, fc2, slots, rows
    )
    branch_sent = [sent_x, sent_y, sent_d]
    ff_other = tie(ff_other, received)
    ff_theirs = links.core(ff_other)
    ff_sent, ff_own = line_sum(line, ff_mine, ff_theirs)
    grad_middle, grad_branch, sums = middle_back(
        links, own, received, middle, got[0], out_grad, small_f, slots, count
    )
    branch_got = [links.rep(v, k) for k, v in enumerate(branch_sent, start=1)]
    grad_branch = tie(grad_branch, branch_got)
    grad_branch = lax.all_gather(grad_branch, "rep", axis=0)
    ff_sum = line_send(links, ff_sent, ff_own)

    attn_mine, attn_other, own, sent_x, sent_y, sent_d = attn_back(
        links,
        grad_branch,
        got,
        proj,
        weights,
        normed_one,
        qkv,
        probs,
        attended,
        sums,
        bias_sums,
        slots,
        rows,
    )
    attn_other = tie(attn_other, ff_sum)
    attn_theirs = links.core(attn_other)
    attn_sent, attn_own = line_sum(line, attn_mine, attn_theirs)
    attn_sent = tie(attn_sent, ff_sum)
    attn_sum = line_send(links, attn_sent, attn_own)

    own_sent = [sent_x, sent_y, sent_d]
    own_got = []
    for k in range(1, 4):
        own_got.append(links.rep(own_sent[k - 1], k))
        own = own + own_got[-1].astype(F32)
        branch = branch + branch_got[k - 1].astype(F32)
    live = (jnp.arange(slots) < jnp.sum(lengths)).astype(F32)[:, None]
    mixed_out = ((middle + branch + small_f[7]) * live).astype(LOW)
    unit_rows, scale = unit(tokens.astype(F32))
    grad_tokens = grad_middle + norm_back(own, small_f[0], unit_rows, scale)

    fc_out, fc2_out = ff_results(links, links.rep_gather(tie(ff_sum.astype(LOW), own_got)), rows)
    qkv_out, proj_out, gains_out, shifts_out, bias_out = attn_results(
        links, lax.all_gather(attn_sum.astype(LOW), "rep", axis=0), rows
    )
    return (
        mixed_out,
        grad_tokens,
        gains_out,
        shifts_out,
        qkv_out,
        proj_out,
        fc_out,
        bias_out,
        fc2_out,
    )


def solution(mesh):
    return jax.shard_map(
        local,
        mesh=mesh,
        in_specs=(
            P(("rep", "shard"), None),
            P(("rep", "shard"), None),
            P(("rep", "shard"), None),
            P(None, "shard"),
            P(None, "shard"),
            P("shard", None),
            P("shard", None),
            P("shard", None),
            P("shard"),
            P("shard", None),
        ),
        out_specs=(
            P(("rep", "shard"), None),
            P(("rep", "shard"), None),
            P(None, "shard"),
            P(None, "shard"),
            P("shard", None),
            P("shard", None),
            P("shard", None),
            P("shard"),
            P("shard", None),
        ),
        check_vma=False,
    )
```

```python
from functools import partial

import jax
import jax.numpy as jnp
from jax import lax
from jax.experimental import pallas as pl
from jax.experimental.pallas import tpu as pltpu
from jax.sharding import PartitionSpec as P

HEAD_DIM = 64
EPS = 1e-05
LOW = jnp.bfloat16
F32 = jnp.float32


def normalize(values, gain_row, shift_row):
    row_mean = jnp.mean(values, axis=-1, keepdims=True)
    centered = values - row_mean
    variance = jnp.mean(centered * centered, axis=-1, keepdims=True)
    return centered * lax.rsqrt(variance + EPS) * gain_row + shift_row


def contract(left_rows, right_rows):
    return lax.dot_general(
        left_rows, right_rows, (((0,), (0,)), ((), ())), preferred_element_type=F32
    )


def back_mult(grad_rows, weight):
    return lax.dot_general(
        grad_rows, weight, (((1,), (1,)), ((), ())), preferred_element_type=F32
    )


def mult(left, right):
    return jnp.dot(left, right, preferred_element_type=F32)


class Links:
    def __init__(self):
        self.shards = lax.axis_size("shard")
        self.line = self.shards // 2
        place = lax.axis_index("shard")
        self.z = place // 2
        self.c = place % 2
        self.j = lax.axis_index("rep")
        self.scalars = jnp.stack([self.z, self.c, self.j, place]).astype(jnp.int32)
        assert lax.axis_size("rep") == 4

    def core(self, v):
        return lax.ppermute(v, "shard", [(i, i ^ 1) for i in range(self.shards)])

    def along(self, v, hop):
        n = self.shards
        return lax.ppermute(v, "shard", [(i, (i + 2 * hop) % n) for i in range(n)])

    def rep(self, v, k):
        return lax.ppermute(v, "rep", [(i, i ^ k) for i in range(4)])

    def rep_gather(self, v):
        return [v] + [self.rep(v, k) for k in range(1, 4)]


def pick(stack, index, axis=0):
    return lax.dynamic_index_in_dim(stack, index, axis, keepdims=False)


def run(kernel, out_shapes, scalars, args, scratch=()):
    return pl.pallas_call(
        kernel,
        out_shape=[jax.ShapeDtypeStruct(shape, dtype) for shape, dtype in out_shapes],
        in_specs=[pl.BlockSpec(memory_space=pltpu.SMEM)]
        + [pl.BlockSpec(memory_space=pltpu.VMEM)] * len(args),
        out_specs=[pl.BlockSpec(memory_space=pltpu.VMEM)] * len(out_shapes),
        scratch_shapes=list(scratch),
        compiler_params=pltpu.CompilerParams(vmem_limit_bytes=56 * 1024 * 1024),
        cost_estimate=pl.CostEstimate(flops=1, bytes_accessed=1, transcendentals=0),
    )(scalars, *args)


def tie(value, *others):
    return lax.optimization_barrier((value, others))[0]


def line_gather(links, block, end=None):
    return [block] + [links.along(block, hop) for hop in range(1, end or links.line)]


def with_partners(links, mine):
    return mine + [links.core(v) for v in mine]


def assemble(scalar_ref, refs, out, start, rows):
    line = len(refs) // 2
    z, c = scalar_ref[0], scalar_ref[1]
    for hop in range(line):
        at = lax.rem(z + line - hop, line)
        for side in range(2):
            to = (2 * at + c) if side == 0 else (2 * at + 1 - c)
            block = refs[side * line + hop][pl.ds(start, rows), :]
            if rows % 16 == 0:
                out[pl.ds(pl.multiple_of(to * rows, 16), rows), :] = block
                continue
            for s in range(2 * line):

                @pl.when(to == s)
                def _(block=block, s=s):
                    out[s * rows : (s + 1) * rows, :] = block


def store_pieces(scalar_ref, scratch, first, outs, start):
    mine, other = outs
    rows = scratch.shape[1]
    line = scratch.shape[0] // 2
    pitch = mine.shape[0] // line
    for s in range(2 * line):
        scratch[s] = first[s * rows : (s + 1) * rows]
    z, c = scalar_ref[0], scalar_ref[1]
    for hop in range(line):
        at = 2 * lax.rem(z + hop, line)
        to = pl.ds(hop * pitch + start, rows)
        mine[to, :] = scratch[at + c].astype(LOW)
        other[to, :] = scratch[at + 1 - c].astype(LOW)


def line_sum(line, mine, theirs):
    rows = mine.shape[0] // line
    both = [
        mine[hop * rows : (hop + 1) * rows].astype(F32)
        + theirs[hop * rows : (hop + 1) * rows].astype(F32)
        for hop in range(line)
    ]
    return [v.astype(LOW) for v in both[1:]], both[0]


def line_send(links, sent, own):
    for hop, value in enumerate(sent, start=1):
        own = own + links.along(value, hop).astype(F32)
    return own


def pad_rows(v, rows):
    return v if v.shape[0] == rows else jnp.pad(v, ((0, rows - v.shape[0]), (0, 0)))


def unit(values):
    row_mean = jnp.mean(values, axis=-1, keepdims=True)
    centered = values - row_mean
    variance = jnp.mean(centered * centered, axis=-1, keepdims=True)
    scale = lax.rsqrt(variance + EPS)
    return centered * scale, scale


def norm_back(cotangent, gain, unit_rows, scale):
    weighted = cotangent * gain
    return scale * (
        weighted
        - jnp.mean(weighted, axis=-1, keepdims=True)
        - unit_rows * jnp.mean(weighted * unit_rows, axis=-1, keepdims=True)
    )


def gelu_pair(x):
    root = 0.7978845608028654
    square = x * x
    bend = jnp.tanh(root * x * (1.0 + 0.044715 * square))
    half = 0.5 * (1.0 + bend)
    slope = half + 0.5 * x * (1.0 - bend * bend) * root * (1.0 + 3 * 0.044715 * square)
    return x * half, slope


def choose(index, options):
    value = options[0]
    for k in range(1, len(options)):
        value = jnp.where(index == k, options[k], value)
    return value


def live_rows(got, slots, count):
    total = jnp.zeros((1, 1), F32)
    for s in range(count):
        total = total + got[slots : slots + 1, s : s + 1].astype(F32)
    place = lax.broadcasted_iota(jnp.int32, (slots, 1), 0).astype(F32)
    return (place < total).astype(F32)


def pack_attn(links, args, rows, part, full):
    gains, shifts, bias, w_qkv, w_proj = args
    model = w_proj.shape[1]

    def kernel(scalar_ref, gain, shift, bias_ref, qkv_ref, p_ref, out):
        j, s_here = scalar_ref[2], scalar_ref[3]
        for t in range(3):
            out[pl.ds(0, rows), t * part : (t + 1) * part] = choose(
                j,
                [
                    qkv_ref[:, t * model + p * part : t * model + (p + 1) * part]
                    for p in range(4)
                ],
            )
        out[pl.ds(0, rows), 3 * part :] = choose(
            j, [p_ref[:, p * part : (p + 1) * part] for p in range(4)]
        )
        bias_row = bias_ref[...].reshape(1, 4 * rows)
        mine = choose(j, [bias_row[:, p * rows : (p + 1) * rows] for p in range(4)])
        small = jnp.concatenate(
            [v.astype(F32) for v in (gain[...], shift[...], mine)] + [jnp.zeros((7, rows), F32)]
        )
        small = jnp.concatenate([small] * links.shards, axis=1)
        lane = lax.broadcasted_iota(jnp.int32, small.shape, 1)
        here = (lane >= s_here * rows) & (lane < (s_here + 1) * rows)
        out[pl.ds(full, 16), :] = jnp.where(here, small, 0.0).astype(LOW)

    return run(kernel, [((full + 16, model), LOW)], links.scalars, args)[0]


def pack_slots(links, tokens, lengths):
    slots, model = tokens.shape
    count = lengths.shape[1]

    def kernel(scalar_ref, tok, len_ref, sent):
        sent[pl.ds(0, slots), :] = tok[...]
        sent[pl.ds(slots, 16), :] = jnp.zeros((16, model), LOW)
        sent[slots : slots + 1, :count] = len_ref[...].astype(F32).astype(LOW)

    shapes = [((slots + 16, model), LOW)]
    return run(kernel, shapes, links.scalars, [tokens, lengths])[0]


def pack_ff(links, w_fc, w_fc2, rows, full):
    model = w_fc2.shape[1]

    def kernel(scalar_ref, fc_ref, fc2_ref, out):
        j = scalar_ref[2]
        for s in range(links.shards):
            out[pl.ds(0, rows), s * rows : (s + 1) * rows] = choose(
                j,
                [fc_ref[:, (4 * s + p) * rows : (4 * s + p + 1) * rows] for p in range(4)],
            )
        out[pl.ds(full, rows), :] = choose(
            j, [fc2_ref[p * rows : (p + 1) * rows, :] for p in range(4)]
        )

    return run(kernel, [((full + rows, model), LOW)], links.scalars, [w_fc, w_fc2])[0]


def proj_lanes(links, blocks, out_grad, rows, part):
    model = blocks[0].shape[1]
    line = links.line

    def kernel(scalar_ref, *refs):
        ins, cot, mine, other, scratch = refs[:-4], *refs[-4:]
        mine[pl.ds(part // 2, cot.shape[0]), :] = cot[...]
        assemble(scalar_ref, [ref.at[:, pl.ds(512, 256)] for ref in ins], scratch, 0, rows)
        c = scalar_ref[1]
        for out, side in ((mine, c), (other, 1 - c)):
            for g in range(4):
                at = pl.ds(pl.multiple_of(g * part + side * (part // 2), 16), part // 2)
                out[pl.ds(0, part // 2), g * part : (g + 1) * part] = scratch[at, 64:]

    shapes = [((part // 2 + out_grad.shape[0], model), LOW), ((part // 2, model), LOW)]
    scratch = [pltpu.VMEM((model, 256), LOW)]
    return run(kernel, shapes, links.scalars, [*blocks, out_grad], scratch)


def attn_forward(links, got, blocks, slots, heads, count, rows):
    model = blocks[0].shape[1]
    part = heads * HEAD_DIM
    full = -(-rows // 16) * 16

    def kernel(scalar_ref, *refs):
        ins, parts = refs[:4], refs[4 : 4 + len(blocks)]
        w_ref, unit_out, qkv_out, probs_out, sent_out, small_out = refs[4 + len(blocks) :]
        j = scalar_ref[2]
        assemble(scalar_ref, parts, w_ref, 0, rows)
        small_sum = jnp.zeros(small_out.shape, F32)
        for ref in parts:
            small_sum = small_sum + ref[pl.ds(full, 16), :].astype(F32)
        small_out[...] = small_sum
        cut = lambda row: choose(
            j, [small_sum[row : row + 1, p * part : (p + 1) * part] for p in range(4)]
        )
        q_bias, v_bias = cut(4), cut(5)
        rows_at = lax.broadcasted_iota(jnp.int32, (slots, slots), 0).astype(F32)
        cols_at = lax.broadcasted_iota(jnp.int32, (slots, slots), 1).astype(F32)
        for k in range(4):
            normed = unit(ins[k][:slots].astype(F32))[0] * small_sum[0:1] + small_sum[2:3]
            unit_out[k * slots : (k + 1) * slots] = normed.astype(LOW)
        qkv = mult(unit_out[...], w_ref[:, : 3 * part])
        qkv_out[:, :part] = (qkv[:, :part] + q_bias).astype(LOW)
        qkv_out[:, part : 2 * part] = qkv[:, part : 2 * part].astype(LOW)
        qkv_out[:, 2 * part :] = (qkv[:, 2 * part :] + v_bias).astype(LOW)
        for k in range(4):
            block = slice(k * slots, (k + 1) * slots)
            end = jnp.zeros((1, 1), F32)
            row_seq, col_seq = jnp.zeros((slots, slots), F32), jnp.zeros((slots, slots), F32)
            for s in range(count):
                end = end + ins[k][slots : slots + 1, s : s + 1].astype(F32)
                row_seq = row_seq + (end <= rows_at).astype(F32)
                col_seq = col_seq + (end <= cols_at).astype(F32)
            allowed = (row_seq == col_seq) & (cols_at <= rows_at)
            for h in range(heads):
                at = h * HEAD_DIM
                query = qkv_out[block, at : at + HEAD_DIM]
                keys = qkv_out[block, part + at : part + at + HEAD_DIM]
                values = qkv_out[block, 2 * part + at : 2 * part + at + HEAD_DIM]
                scores = back_mult(query, keys) * (HEAD_DIM**-0.5)
                scores = jnp.where(allowed, scores, -1000000000.0)
                exponent = jnp.exp(scores - jnp.max(scores, axis=-1, keepdims=True))
                probs = exponent / jnp.sum(exponent, axis=-1, keepdims=True)
                probs_out[k, h] = probs
                attended = mult(probs.astype(LOW), values)
                to = k * part + at
                sent_out[:, to : to + HEAD_DIM] = attended.astype(LOW)

    shapes = [
        ((model, model), LOW),
        ((4 * slots, model), LOW),
        ((4 * slots, 3 * part), LOW),
        ((4, heads, slots, slots), F32),
        ((slots, 4 * part), LOW),
        ((16, model), F32),
    ]
    return run(kernel, shapes, links.scalars, [*got, *blocks])


def ff_both(links, got, attended, proj, blocks, small, slots, count, rows):
    model = blocks[0].shape[1]
    part = model // 4
    full = -(-rows // 16) * 16
    held = 4 + 1 + 8 + len(blocks) + 1

    def kernel(scalar_ref, *refs):
        ins, att, p_parts, parts, small_ref = (
            refs[:4],
            refs[4],
            refs[5:13],
            refs[13 : held - 1],
            refs[held - 1],
        )
        att_out, middle_out, normed_out, active_out, hidden_out, cot_out = refs[held : held + 6]
        own_out, *sent_out = refs[held + 6 : held + 10]
        sums_out, p_ref, fc2_ref, fc_ref = refs[held + 10 :]
        c, j = scalar_ref[1], scalar_ref[2]
        assemble(scalar_ref, parts, fc_ref, 0, rows)
        assemble(scalar_ref, parts, fc2_ref, full, rows)
        for p in range(4):
            for g in range(4):
                for side, half in ((c, p_parts[:4]), (1 - c, p_parts[4:])):
                    at = pl.ds(pl.multiple_of(g * part + side * (part // 2), 16), part // 2)
                    p_ref[at, p * part : (p + 1) * part] = choose(
                        j ^ p, [ref[: part // 2, g * part : (g + 1) * part] for ref in half]
                    )
        total = jnp.zeros((1, model), F32)
        for k in range(4):
            for p in range(4):
                att_out[k * slots : (k + 1) * slots, p * part : (p + 1) * part] = choose(
                    j ^ p, [att[p, :, (k ^ m) * part : ((k ^ m) + 1) * part] for m in range(4)]
                )
        for first in (0, 2):
            both = (first, first + 1)
            block = slice(first * slots, (first + 2) * slots)
            middle = jnp.concatenate([ins[k][:slots].astype(F32) for k in both])
            middle = middle + mult(att_out[block], p_ref[...]) + small_ref[6:7]
            if first == 0:
                middle_out[...] = middle[:slots]
            normed = (unit(middle)[0] * small_ref[1:2] + small_ref[3:4]).astype(LOW)
            normed_out[block] = normed
            hidden = mult(normed, fc_ref[...]) + small_ref[8:9]
            active, slope = gelu_pair(hidden)
            active_out[block] = active.astype(LOW)
            cot = jnp.concatenate(
                [
                    p_parts[k][part // 2 :].astype(F32) * live_rows(ins[k], slots, count)
                    for k in both
                ]
            ).astype(LOW)
            cot_out[block] = cot
            grad_hidden = (back_mult(cot, fc2_ref[...]) * slope).astype(LOW)
            hidden_out[block] = grad_hidden
            total = total + jnp.sum(grad_hidden.astype(F32), axis=0, keepdims=True)
            grad_normed = back_mult(grad_hidden, fc_ref[...])
            for k in both:
                grad_rows = grad_normed[(k - first) * slots : (k - first + 1) * slots]
                if k == 0:
                    own_out[...] = grad_rows
                else:
                    sent_out[k - 1][...] = grad_rows.astype(LOW)
        sums_out[...] = total

    shapes = [
        ((4 * slots, model), LOW),
        ((slots, model), F32),
        ((4 * slots, model), LOW),
        ((4 * slots, model), LOW),
        ((4 * slots, model), LOW),
        ((4 * slots, model), LOW),
        ((slots, model), F32),
        *[((slots, model), LOW)] * 3,
        ((1, model), F32),
        ((model, model), LOW),
        ((model, model), LOW),
    ]
    args = [*got, attended, *proj, *blocks, small]
    return run(kernel, shapes, links.scalars, args, [pltpu.VMEM((model, model), LOW)])


def ff_grads(links, normed, active, hidden, cot, fc2, slots, rows):
    model = normed.shape[1]
    line = links.line
    full = -(-rows // 16) * 16

    def kernel(scalar_ref, *refs):
        normed_ref, active_ref, hidden_ref, cot_ref, fc2_ref = refs[:5]
        pieces = refs[5:7]
        branch_own, *branch_sent, scratch = refs[7:]
        for start, left, right in ((0, normed_ref, hidden_ref), (full, active_ref, cot_ref)):
            store_pieces(scalar_ref, scratch, contract(left[...], right[...]), pieces, start)
        branch = mult(active_ref[...], fc2_ref[...])
        branch_own[...] = branch[:slots]
        for k in range(1, 4):
            branch_sent[k - 1][...] = branch[k * slots : (k + 1) * slots].astype(LOW)

    shapes = [
        *[((line * (full + rows), model), LOW)] * 2,
        ((slots, model), F32),
        *[((slots, model), LOW)] * 3,
    ]
    args = [normed, active, hidden, cot, fc2]
    return run(kernel, shapes, links.scalars, args, [pltpu.VMEM((2 * line, rows, model), F32)])


def middle_back(links, own, received, middle, got, out_grad, small, slots, count):
    def kernel(scalar_ref, own_ref, r1, r2, r3, middle_ref, got_ref, cot_ref, small_ref, *outs):
        grad_out, branch_out, sums_out = outs
        cotangent = own_ref[...] + r1[...].astype(F32) + r2[...].astype(F32) + r3[...].astype(F32)
        unit_rows, scale = unit(middle_ref[...])
        live = live_rows(got_ref, slots, count)
        cot = cot_ref[...].astype(F32) * live
        grad = cot + norm_back(cotangent, small_ref[1:2], unit_rows, scale)
        grad_out[...] = grad
        branch = grad.astype(LOW)
        branch_out[...] = branch
        sums_out[0:1] = jnp.sum(cotangent * unit_rows, axis=0, keepdims=True)
        sums_out[1:2] = jnp.sum(cotangent, axis=0, keepdims=True)
        sums_out[2:3] = jnp.sum(branch.astype(F32), axis=0, keepdims=True)
        sums_out[3:4] = jnp.sum(cot, axis=0, keepdims=True)

    model = own.shape[1]
    shapes = [((slots, model), F32), ((slots, model), LOW), ((4, model), F32)]
    return run(kernel, shapes, links.scalars, [own, *received, middle, got, out_grad, small])


def attn_back(
    links,
    grads,
    got,
    proj,
    weights,
    normed,
    qkv,
    probs,
    attended,
    sums,
    bias,
    slots,
    rows,
):
    model = normed.shape[1]
    heads = probs.shape[1]
    part = heads * HEAD_DIM
    line = links.line
    full = -(-rows // 16) * 16
    scale = HEAD_DIM**-0.5

    def kernel(scalar_ref, *refs):
        grad_ref, ins = refs[0], refs[1:5]
        p_ref, w_ref, normed_ref, qkv_ref, probs_ref, att_ref, sums_ref, bias_ref = refs[5:13]
        pieces = refs[13:15]
        own_out, *sent_out, scratch, grad_qkv, branch, cols = refs[15:]
        j = scalar_ref[2]
        for k in range(4):
            block = slice(k * slots, (k + 1) * slots)
            branch[block] = grad_ref[j ^ k]
            cols[block] = choose(
                j, [grad_ref[j ^ k, :, p * part : (p + 1) * part] for p in range(4)]
            )
        proj_rows = p_ref[pl.ds(pl.multiple_of(j * part, part), part), :]
        grad_att = back_mult(branch[...], proj_rows).astype(LOW)
        for k in range(4):
            block = slice(k * slots, (k + 1) * slots)
            for h in range(heads):
                at = h * HEAD_DIM
                query = qkv_ref[block, at : at + HEAD_DIM]
                keys = qkv_ref[block, part + at : part + at + HEAD_DIM]
                values = qkv_ref[block, 2 * part + at : 2 * part + at + HEAD_DIM]
                prob = probs_ref[k, h]
                cot = grad_att[block, at : at + HEAD_DIM]
                grad_probs = back_mult(cot, values)
                inner = jnp.sum(prob * grad_probs, axis=-1, keepdims=True)
                grad_scores = (prob * (grad_probs - inner)).astype(LOW)
                grad_qkv[block, at : at + HEAD_DIM] = (mult(grad_scores, keys) * scale).astype(LOW)
                grad_qkv[block, part + at : part + at + HEAD_DIM] = (
                    contract(grad_scores, query) * scale
                ).astype(LOW)
                grad_qkv[block, 2 * part + at : 2 * part + at + HEAD_DIM] = contract(
                    prob.astype(LOW), cot
                ).astype(LOW)
        grad_rows = grad_qkv[...]
        qkv_sum = jnp.sum(grad_rows.astype(F32), axis=0, keepdims=True)
        grad_normed = back_mult(grad_rows, w_ref[:, : 3 * part])
        own_out[...] = grad_normed[:slots]
        for k in range(1, 4):
            sent_out[k - 1][...] = grad_normed[k * slots : (k + 1) * slots].astype(LOW)
        gain_sum = jnp.zeros((1, model), F32)
        for k in range(4):
            unit_rows = unit(ins[k][:slots].astype(F32))[0]
            block = slice(k * slots, (k + 1) * slots)
            gain_sum = gain_sum + jnp.sum(grad_normed[block] * unit_rows, axis=0, keepdims=True)
        shift_sum = jnp.sum(grad_normed, axis=0, keepdims=True)
        total = jnp.concatenate(
            [contract(normed_ref[...], grad_rows), contract(att_ref[...], cols[...])], axis=1
        )
        store_pieces(scalar_ref, scratch, total, pieces, 0)
        spread = lambda v: jnp.concatenate(
            [jnp.where(j == p, v, jnp.zeros_like(v)) for p in range(4)], axis=1
        )
        vectors = jnp.concatenate(
            [
                gain_sum,
                sums_ref[0:1],
                shift_sum,
                sums_ref[1:2],
                spread(qkv_sum[:, :part]),
                spread(qkv_sum[:, 2 * part :]),
                sums_ref[2:4],
                bias_ref[...],
                jnp.zeros((7, model), F32),
            ]
        ).astype(LOW)
        for out in pieces:
            for hop in range(line):
                out[pl.ds(hop * (full + 16) + full, 16), :] = vectors

    shapes = [
        *[((line * (full + 16), model), LOW)] * 2,
        ((slots, model), F32),
        *[((slots, model), LOW)] * 3,
    ]
    args = [grads, *got, proj, weights, normed, qkv, probs, attended, sums, bias]
    scratch = [
        pltpu.VMEM((2 * line, rows, model), F32),
        pltpu.VMEM((4 * slots, 3 * part), LOW),
        pltpu.VMEM((4 * slots, model), LOW),
        pltpu.VMEM((4 * slots, part), LOW),
    ]
    return run(kernel, shapes, links.scalars, args, scratch)


def ff_results(links, parts, rows):
    model = parts[0].shape[1]
    shards = links.shards
    full = -(-rows // 16) * 16

    def kernel(scalar_ref, *refs):
        ins, fc_out, fc2_out = refs[:4], refs[4], refs[5]
        j = scalar_ref[2]
        for p in range(4):
            left = choose(j ^ p, [ref[pl.ds(0, rows), :] for ref in ins]).astype(F32)
            for s in range(shards):
                at = (s * 4 + p) * rows
                fc_out[:, at : at + rows] = left[:, s * rows : (s + 1) * rows]
            fc2_out[pl.ds(p * rows, rows), :] = choose(
                j ^ p, [ref[pl.ds(full, rows), :] for ref in ins]
            ).astype(F32)

    shapes = [((rows, 4 * model), F32), ((4 * rows, model), F32)]
    return run(kernel, shapes, links.scalars, parts)


def attn_results(links, got, rows):
    model = got.shape[2]
    shards = links.shards
    part = model // 4
    full = -(-rows // 16) * 16

    def kernel(scalar_ref, *refs):
        got_ref, qkv_out, proj_out, gains_out, shifts_out, bias_out = refs
        s_here = scalar_ref[3]
        for p in range(4):
            block = got_ref[p, pl.ds(0, rows), :].astype(F32)
            for t in range(3):
                at = t * model + p * part
                qkv_out[:, at : at + part] = block[:, t * part : (t + 1) * part]
            proj_out[:, p * part : (p + 1) * part] = block[:, 3 * part :]
        cut = lambda v: choose(s_here, [v[:, s * rows : (s + 1) * rows] for s in range(shards)])
        low = [cut(got_ref[p, pl.ds(full, 16), :].astype(F32)) for p in range(4)]
        sums = low[0] + low[1] + low[2] + low[3]
        gains_out[...] = sums[:2]
        shifts_out[...] = sums[2:8]
        bias = jnp.concatenate([v[8:9] for v in low], axis=1)
        bias_out[...] = bias.reshape(bias_out.shape)

    shapes = [
        ((rows, 3 * model), F32),
        ((rows, model), F32),
        ((2, rows), F32),
        ((6, rows), F32),
        ((4 * rows,), F32),
    ]
    return run(kernel, shapes, links.scalars, [got])


def local(tokens, out_grad, lengths, gains, shifts, w_qkv, w_proj, w_fc, bias_fc, w_fc2):
    links = Links()
    line, shards = links.line, links.shards
    z, c, j = links.z, links.c, links.j
    slots, model = tokens.shape
    count = lengths.shape[1]
    rows = w_proj.shape[0]
    quarter = w_fc2.shape[0] // 4
    assert quarter == rows and w_fc.shape[1] == 4 * model
    heads = model // HEAD_DIM // 4
    part = heads * HEAD_DIM
    full_rows = -(-rows // 16) * 16

    attn_block = pack_attn(links, [gains, shifts, bias_fc, w_qkv, w_proj], rows, part, full_rows)
    sent = pack_slots(links, tie(tokens, attn_block), lengths)
    w_fc, w_fc2 = tie((w_fc, w_fc2), sent)
    ff_block = pack_ff(links, w_fc, w_fc2, rows, full_rows)

    attn_mine = line_gather(links, attn_block)
    got = links.rep_gather(sent)
    attn_mine, got, ff_block = lax.optimization_barrier((attn_mine, got, ff_block))
    attn_blocks = with_partners(links, attn_mine)
    ff_mine = line_gather(links, ff_block, links.line - 1)

    proj_mine, proj_other = proj_lanes(links, attn_blocks, out_grad, rows, part)
    proj = links.rep_gather(proj_mine)
    attn_blocks = tie(attn_blocks, proj_mine)
    weights, normed_one, qkv, probs, sent, small_f = attn_forward(
        links, got, attn_blocks, slots, heads, count, rows
    )
    ff_mine.append(links.along(tie(ff_block, sent), line - 1))
    attended = lax.all_gather(sent, "rep", axis=0)
    proj, ff_mine = tie((proj, ff_mine), attended)
    proj = proj + [proj_other] + [links.core(v) for v in proj[1:]]
    ff_blocks = with_partners(links, ff_mine)
    (
        attended,
        middle,
        normed_two,
        active,
        grad_hidden,
        cot,
        own,
        sent_x,
        sent_y,
        sent_d,
        bias_sums,
        proj,
        fc2,
    ) = ff_both(links, got, attended, proj, ff_blocks, small_f, slots, count, rows)
    received = [links.rep(v, k) for k, v in ((1, sent_x), (2, sent_y), (3, sent_d))]
    ff_mine, ff_other, branch, sent_x, sent_y, sent_d = ff_grads(
        links, normed_two, active, grad_hidden, cot, fc2, slots, rows
    )
    branch_sent = [sent_x, sent_y, sent_d]
    ff_other = tie(ff_other, received)
    ff_theirs = links.core(ff_other)
    ff_sent, ff_own = line_sum(line, ff_mine, ff_theirs)
    grad_middle, grad_branch, sums = middle_back(
        links, own, received, middle, got[0], out_grad, small_f, slots, count
    )
    ff_sent = tie(ff_sent, grad_branch)
    branch_got = [links.rep(v, k) for k, v in enumerate(branch_sent, start=1)]
    grad_branch = tie(grad_branch, branch_got)
    grad_branch = lax.all_gather(grad_branch, "rep", axis=0)
    ff_sum = line_send(links, ff_sent, ff_own)

    attn_mine, attn_other, own, sent_x, sent_y, sent_d = attn_back(
        links,
        grad_branch,
        got,
        proj,
        weights,
        normed_one,
        qkv,
        probs,
        attended,
        sums,
        bias_sums,
        slots,
        rows,
    )
    attn_other = tie(attn_other, ff_sum)
    attn_theirs = links.core(attn_other)
    attn_sent, attn_own = line_sum(line, attn_mine, attn_theirs)
    attn_sent = tie(attn_sent, ff_sum)
    attn_sum = line_send(links, attn_sent, attn_own)

    own_sent = [sent_x, sent_y, sent_d]
    own_got = []
    for k in range(1, 4):
        own_got.append(links.rep(own_sent[k - 1], k))
        own = own + own_got[-1].astype(F32)
        branch = branch + branch_got[k - 1].astype(F32)
    live = (jnp.arange(slots) < jnp.sum(lengths)).astype(F32)[:, None]
    mixed_out = ((middle + branch + small_f[7]) * live).astype(LOW)
    unit_rows, scale = unit(tokens.astype(F32))
    grad_tokens = grad_middle + norm_back(own, small_f[0], unit_rows, scale)

    fc_out, fc2_out = ff_results(links, links.rep_gather(tie(ff_sum.astype(LOW), own_got)), rows)
    qkv_out, proj_out, gains_out, shifts_out, bias_out = attn_results(
        links, lax.all_gather(attn_sum.astype(LOW), "rep", axis=0), rows
    )
    return (
        mixed_out,
        grad_tokens,
        gains_out,
        shifts_out,
        qkv_out,
        proj_out,
        fc_out,
        bias_out,
        fc2_out,
    )


def solution(mesh):
    return jax.shard_map(
        local,
        mesh=mesh,
        in_specs=(
            P(("rep", "shard"), None),
            P(("rep", "shard"), None),
            P(("rep", "shard"), None),
            P(None, "shard"),
            P(None, "shard"),
            P("shard", None),
            P("shard", None),
            P("shard", None),
            P("shard"),
            P("shard", None),
        ),
        out_specs=(
            P(("rep", "shard"), None),
            P(("rep", "shard"), None),
            P(None, "shard"),
            P(None, "shard"),
            P("shard", None),
            P("shard", None),
            P("shard", None),
            P("shard"),
            P("shard", None),
        ),
        check_vma=False,
    )
```

```python
from functools import partial

import jax
import jax.numpy as jnp
from jax import lax
from jax.experimental import pallas as pl
from jax.experimental.pallas import tpu as pltpu
from jax.sharding import PartitionSpec as P

HEAD_DIM = 64
EPS = 1e-05
LOW = jnp.bfloat16
F32 = jnp.float32


def normalize(values, gain_row, shift_row):
    row_mean = jnp.mean(values, axis=-1, keepdims=True)
    centered = values - row_mean
    variance = jnp.mean(centered * centered, axis=-1, keepdims=True)
    return centered * lax.rsqrt(variance + EPS) * gain_row + shift_row


def contract(left_rows, right_rows):
    return lax.dot_general(
        left_rows, right_rows, (((0,), (0,)), ((), ())), preferred_element_type=F32
    )


def back_mult(grad_rows, weight):
    return lax.dot_general(
        grad_rows, weight, (((1,), (1,)), ((), ())), preferred_element_type=F32
    )


def mult(left, right):
    return jnp.dot(left, right, preferred_element_type=F32)


class Links:
    def __init__(self):
        self.shards = lax.axis_size("shard")
        self.line = self.shards // 2
        place = lax.axis_index("shard")
        self.z = place // 2
        self.c = place % 2
        self.j = lax.axis_index("rep")
        self.scalars = jnp.stack([self.z, self.c, self.j, place]).astype(jnp.int32)
        assert lax.axis_size("rep") == 4

    def core(self, v):
        return lax.ppermute(v, "shard", [(i, i ^ 1) for i in range(self.shards)])

    def along(self, v, hop):
        n = self.shards
        return lax.ppermute(v, "shard", [(i, (i + 2 * hop) % n) for i in range(n)])

    def rep(self, v, k):
        return lax.ppermute(v, "rep", [(i, i ^ k) for i in range(4)])

    def rep_gather(self, v):
        return [v] + [self.rep(v, k) for k in range(1, 4)]


def pick(stack, index, axis=0):
    return lax.dynamic_index_in_dim(stack, index, axis, keepdims=False)


def run(kernel, out_shapes, scalars, args, scratch=()):
    return pl.pallas_call(
        kernel,
        out_shape=[jax.ShapeDtypeStruct(shape, dtype) for shape, dtype in out_shapes],
        in_specs=[pl.BlockSpec(memory_space=pltpu.SMEM)]
        + [pl.BlockSpec(memory_space=pltpu.VMEM)] * len(args),
        out_specs=[pl.BlockSpec(memory_space=pltpu.VMEM)] * len(out_shapes),
        scratch_shapes=list(scratch),
        compiler_params=pltpu.CompilerParams(vmem_limit_bytes=56 * 1024 * 1024),
        cost_estimate=pl.CostEstimate(flops=1, bytes_accessed=1, transcendentals=0),
    )(scalars, *args)


def tie(value, *others):
    return lax.optimization_barrier((value, others))[0]


def line_gather(links, block, end=None):
    return [block] + [links.along(block, hop) for hop in range(1, end or links.line)]


def with_partners(links, mine, own_theirs=None):
    theirs = [links.core(v) for v in mine[1:]]
    return mine + [links.core(mine[0]) if own_theirs is None else own_theirs] + theirs


def assemble(scalar_ref, refs, out, start, rows):
    line = len(refs) // 2
    z, c = scalar_ref[0], scalar_ref[1]
    for hop in range(line):
        at = lax.rem(z + line - hop, line)
        for side in range(2):
            to = (2 * at + c) if side == 0 else (2 * at + 1 - c)
            block = refs[side * line + hop][pl.ds(start, rows), :]
            if rows % 16 == 0:
                out[pl.ds(pl.multiple_of(to * rows, 16), rows), :] = block
                continue
            for s in range(2 * line):

                @pl.when(to == s)
                def _(block=block, s=s):
                    out[s * rows : (s + 1) * rows, :] = block


def store_pieces(scalar_ref, scratch, first, outs, start):
    mine, other = outs
    rows = scratch.shape[1]
    line = scratch.shape[0] // 2
    pitch = mine.shape[0] // line
    for s in range(2 * line):
        scratch[s] = first[s * rows : (s + 1) * rows]
    z, c = scalar_ref[0], scalar_ref[1]
    for hop in range(line):
        at = 2 * lax.rem(z + hop, line)
        to = pl.ds(hop * pitch + start, rows)
        mine[to, :] = scratch[at + c].astype(LOW)
        other[to, :] = scratch[at + 1 - c].astype(LOW)


def line_sum(line, mine, theirs):
    rows = mine.shape[0] // line
    both = [
        mine[hop * rows : (hop + 1) * rows].astype(F32)
        + theirs[hop * rows : (hop + 1) * rows].astype(F32)
        for hop in range(line)
    ]
    return [v.astype(LOW) for v in both[1:]], both[0]


def line_send(links, sent, own):
    for hop, value in enumerate(sent, start=1):
        own = own + links.along(value, hop).astype(F32)
    return own


def pad_rows(v, rows):
    return v if v.shape[0] == rows else jnp.pad(v, ((0, rows - v.shape[0]), (0, 0)))


def unit(values):
    row_mean = jnp.mean(values, axis=-1, keepdims=True)
    centered = values - row_mean
    variance = jnp.mean(centered * centered, axis=-1, keepdims=True)
    scale = lax.rsqrt(variance + EPS)
    return centered * scale, scale


def norm_back(cotangent, gain, unit_rows, scale):
    weighted = cotangent * gain
    return scale * (
        weighted
        - jnp.mean(weighted, axis=-1, keepdims=True)
        - unit_rows * jnp.mean(weighted * unit_rows, axis=-1, keepdims=True)
    )


def gelu_pair(x):
    root = 0.7978845608028654
    square = x * x
    bend = jnp.tanh(root * x * (1.0 + 0.044715 * square))
    half = 0.5 * (1.0 + bend)
    slope = half + 0.5 * x * (1.0 - bend * bend) * root * (1.0 + 3 * 0.044715 * square)
    return x * half, slope


def choose(index, options):
    value = options[0]
    for k in range(1, len(options)):
        value = jnp.where(index == k, options[k], value)
    return value


def live_rows(got, slots, count):
    total = jnp.zeros((1, 1), F32)
    for s in range(count):
        total = total + got[slots : slots + 1, s : s + 1].astype(F32)
    place = lax.broadcasted_iota(jnp.int32, (slots, 1), 0).astype(F32)
    return (place < total).astype(F32)


def pack_attn(links, args, rows, part, full):
    gains, shifts, bias, w_qkv, w_proj = args
    model = w_proj.shape[1]

    def kernel(scalar_ref, gain, shift, bias_ref, qkv_ref, p_ref, out):
        j, s_here = scalar_ref[2], scalar_ref[3]
        for t in range(3):
            out[pl.ds(0, rows), t * part : (t + 1) * part] = choose(
                j,
                [
                    qkv_ref[:, t * model + p * part : t * model + (p + 1) * part]
                    for p in range(4)
                ],
            )
        out[pl.ds(0, rows), 3 * part :] = choose(
            j, [p_ref[:, p * part : (p + 1) * part] for p in range(4)]
        )
        bias_row = bias_ref[...].reshape(1, 4 * rows)
        mine = choose(j, [bias_row[:, p * rows : (p + 1) * rows] for p in range(4)])
        small = jnp.concatenate(
            [v.astype(F32) for v in (gain[...], shift[...], mine)] + [jnp.zeros((7, rows), F32)]
        )
        small = jnp.concatenate([small] * links.shards, axis=1)
        lane = lax.broadcasted_iota(jnp.int32, small.shape, 1)
        here = (lane >= s_here * rows) & (lane < (s_here + 1) * rows)
        out[pl.ds(full, 16), :] = jnp.where(here, small, 0.0).astype(LOW)

    return run(kernel, [((full + 16, model), LOW)], links.scalars, args)[0]


def pack_slots(links, tokens, lengths):
    slots, model = tokens.shape
    count = lengths.shape[1]

    def kernel(scalar_ref, tok, len_ref, sent):
        sent[pl.ds(0, slots), :] = tok[...]
        sent[pl.ds(slots, 16), :] = jnp.zeros((16, model), LOW)
        sent[slots : slots + 1, :count] = len_ref[...].astype(F32).astype(LOW)

    shapes = [((slots + 16, model), LOW)]
    return run(kernel, shapes, links.scalars, [tokens, lengths])[0]


def pack_ff(links, w_fc, w_fc2, rows, full):
    model = w_fc2.shape[1]

    def kernel(scalar_ref, fc_ref, fc2_ref, out):
        j = scalar_ref[2]
        for s in range(links.shards):
            out[pl.ds(0, rows), s * rows : (s + 1) * rows] = choose(
                j,
                [fc_ref[:, (4 * s + p) * rows : (4 * s + p + 1) * rows] for p in range(4)],
            )
        out[pl.ds(full, rows), :] = choose(
            j, [fc2_ref[p * rows : (p + 1) * rows, :] for p in range(4)]
        )

    return run(kernel, [((full + rows, model), LOW)], links.scalars, [w_fc, w_fc2])[0]


def proj_lanes(links, blocks, out_grad, rows, part):
    model = blocks[0].shape[1]
    line = links.line

    def kernel(scalar_ref, *refs):
        ins, cot, mine, other, scratch = refs[:-4], *refs[-4:]
        mine[pl.ds(part // 2, cot.shape[0]), :] = cot[...]
        assemble(scalar_ref, [ref.at[:, pl.ds(512, 256)] for ref in ins], scratch, 0, rows)
        c = scalar_ref[1]
        for out, side in ((mine, c), (other, 1 - c)):
            for g in range(4):
                at = pl.ds(pl.multiple_of(g * part + side * (part // 2), 16), part // 2)
                out[pl.ds(0, part // 2), g * part : (g + 1) * part] = scratch[at, 64:]

    shapes = [((part // 2 + out_grad.shape[0], model), LOW), ((part // 2, model), LOW)]
    scratch = [pltpu.VMEM((model, 256), LOW)]
    return run(kernel, shapes, links.scalars, [*blocks, out_grad], scratch)


def attn_forward(links, got, blocks, slots, heads, count, rows):
    model = blocks[0].shape[1]
    part = heads * HEAD_DIM
    full = -(-rows // 16) * 16

    def kernel(scalar_ref, *refs):
        ins, parts = refs[:4], refs[4 : 4 + len(blocks)]
        w_ref, unit_out, qkv_out, probs_out, sent_out, small_out = refs[4 + len(blocks) :]
        j = scalar_ref[2]
        assemble(scalar_ref, parts, w_ref, 0, rows)
        small_sum = jnp.zeros(small_out.shape, F32)
        for ref in parts:
            small_sum = small_sum + ref[pl.ds(full, 16), :].astype(F32)
        small_out[...] = small_sum
        cut = lambda row: choose(
            j, [small_sum[row : row + 1, p * part : (p + 1) * part] for p in range(4)]
        )
        q_bias, v_bias = cut(4), cut(5)
        rows_at = lax.broadcasted_iota(jnp.int32, (slots, slots), 0).astype(F32)
        cols_at = lax.broadcasted_iota(jnp.int32, (slots, slots), 1).astype(F32)
        for k in range(4):
            normed = unit(ins[k][:slots].astype(F32))[0] * small_sum[0:1] + small_sum[2:3]
            unit_out[k * slots : (k + 1) * slots] = normed.astype(LOW)
        qkv = mult(unit_out[...], w_ref[:, : 3 * part])
        qkv_out[:, :part] = (qkv[:, :part] + q_bias).astype(LOW)
        qkv_out[:, part : 2 * part] = qkv[:, part : 2 * part].astype(LOW)
        qkv_out[:, 2 * part :] = (qkv[:, 2 * part :] + v_bias).astype(LOW)
        for k in range(4):
            block = slice(k * slots, (k + 1) * slots)
            end = jnp.zeros((1, 1), F32)
            row_seq, col_seq = jnp.zeros((slots, slots), F32), jnp.zeros((slots, slots), F32)
            for s in range(count):
                end = end + ins[k][slots : slots + 1, s : s + 1].astype(F32)
                row_seq = row_seq + (end <= rows_at).astype(F32)
                col_seq = col_seq + (end <= cols_at).astype(F32)
            allowed = (row_seq == col_seq) & (cols_at <= rows_at)
            for h in range(heads):
                at = h * HEAD_DIM
                query = qkv_out[block, at : at + HEAD_DIM]
                keys = qkv_out[block, part + at : part + at + HEAD_DIM]
                values = qkv_out[block, 2 * part + at : 2 * part + at + HEAD_DIM]
                scores = back_mult(query, keys) * (HEAD_DIM**-0.5)
                scores = jnp.where(allowed, scores, -1000000000.0)
                exponent = jnp.exp(scores - jnp.max(scores, axis=-1, keepdims=True))
                probs = exponent / jnp.sum(exponent, axis=-1, keepdims=True)
                probs_out[k, h] = probs
                attended = mult(probs.astype(LOW), values)
                to = k * part + at
                sent_out[:, to : to + HEAD_DIM] = attended.astype(LOW)

    shapes = [
        ((model, model), LOW),
        ((4 * slots, model), LOW),
        ((4 * slots, 3 * part), LOW),
        ((4, heads, slots, slots), F32),
        ((slots, 4 * part), LOW),
        ((16, model), F32),
    ]
    return run(kernel, shapes, links.scalars, [*got, *blocks])


def ff_both(links, got, attended, proj, blocks, small, slots, count, rows):
    model = blocks[0].shape[1]
    part = model // 4
    full = -(-rows // 16) * 16
    held = 4 + 1 + 8 + len(blocks) + 1

    def kernel(scalar_ref, *refs):
        ins, att, p_parts, parts, small_ref = (
            refs[:4],
            refs[4],
            refs[5:13],
            refs[13 : held - 1],
            refs[held - 1],
        )
        att_out, middle_out, normed_out, active_out, hidden_out, cot_out = refs[held : held + 6]
        own_out, *sent_out = refs[held + 6 : held + 10]
        sums_out, p_ref, fc2_ref, fc_ref = refs[held + 10 :]
        c, j = scalar_ref[1], scalar_ref[2]
        assemble(scalar_ref, parts, fc_ref, 0, rows)
        assemble(scalar_ref, parts, fc2_ref, full, rows)
        for p in range(4):
            for g in range(4):
                for side, half in ((c, p_parts[:4]), (1 - c, p_parts[4:])):
                    at = pl.ds(pl.multiple_of(g * part + side * (part // 2), 16), part // 2)
                    p_ref[at, p * part : (p + 1) * part] = choose(
                        j ^ p, [ref[: part // 2, g * part : (g + 1) * part] for ref in half]
                    )
        total = jnp.zeros((1, model), F32)
        for k in range(4):
            for p in range(4):
                att_out[k * slots : (k + 1) * slots, p * part : (p + 1) * part] = choose(
                    j ^ p, [att[p, :, (k ^ m) * part : ((k ^ m) + 1) * part] for m in range(4)]
                )
        for first in (0, 2):
            both = (first, first + 1)
            block = slice(first * slots, (first + 2) * slots)
            middle = jnp.concatenate([ins[k][:slots].astype(F32) for k in both])
            middle = middle + mult(att_out[block], p_ref[...]) + small_ref[6:7]
            if first == 0:
                middle_out[...] = middle[:slots]
            normed = (unit(middle)[0] * small_ref[1:2] + small_ref[3:4]).astype(LOW)
            normed_out[block] = normed
            hidden = mult(normed, fc_ref[...]) + small_ref[8:9]
            active, slope = gelu_pair(hidden)
            active_out[block] = active.astype(LOW)
            cot = jnp.concatenate(
                [
                    p_parts[k][part // 2 :].astype(F32) * live_rows(ins[k], slots, count)
                    for k in both
                ]
            ).astype(LOW)
            cot_out[block] = cot
            grad_hidden = (back_mult(cot, fc2_ref[...]) * slope).astype(LOW)
            hidden_out[block] = grad_hidden
            total = total + jnp.sum(grad_hidden.astype(F32), axis=0, keepdims=True)
            grad_normed = back_mult(grad_hidden, fc_ref[...])
            for k in both:
                grad_rows = grad_normed[(k - first) * slots : (k - first + 1) * slots]
                if k == 0:
                    own_out[...] = grad_rows
                else:
                    sent_out[k - 1][...] = grad_rows.astype(LOW)
        sums_out[...] = total

    shapes = [
        ((4 * slots, model), LOW),
        ((slots, model), F32),
        ((4 * slots, model), LOW),
        ((4 * slots, model), LOW),
        ((4 * slots, model), LOW),
        ((4 * slots, model), LOW),
        ((slots, model), F32),
        *[((slots, model), LOW)] * 3,
        ((1, model), F32),
        ((model, model), LOW),
        ((model, model), LOW),
    ]
    args = [*got, attended, *proj, *blocks, small]
    return run(kernel, shapes, links.scalars, args, [pltpu.VMEM((model, model), LOW)])


def ff_grads(links, normed, active, hidden, cot, fc2, slots, rows):
    model = normed.shape[1]
    line = links.line
    full = -(-rows // 16) * 16

    def kernel(scalar_ref, *refs):
        normed_ref, active_ref, hidden_ref, cot_ref, fc2_ref = refs[:5]
        pieces = refs[5:7]
        branch_own, *branch_sent, scratch = refs[7:]
        for start, left, right in ((0, normed_ref, hidden_ref), (full, active_ref, cot_ref)):
            store_pieces(scalar_ref, scratch, contract(left[...], right[...]), pieces, start)
        branch = mult(active_ref[...], fc2_ref[...])
        branch_own[...] = branch[:slots]
        for k in range(1, 4):
            branch_sent[k - 1][...] = branch[k * slots : (k + 1) * slots].astype(LOW)

    shapes = [
        *[((line * (full + rows), model), LOW)] * 2,
        ((slots, model), F32),
        *[((slots, model), LOW)] * 3,
    ]
    args = [normed, active, hidden, cot, fc2]
    return run(kernel, shapes, links.scalars, args, [pltpu.VMEM((2 * line, rows, model), F32)])


def middle_back(links, own, received, middle, got, out_grad, small, slots, count):
    def kernel(scalar_ref, own_ref, r1, r2, r3, middle_ref, got_ref, cot_ref, small_ref, *outs):
        grad_out, branch_out, sums_out = outs
        cotangent = own_ref[...] + r1[...].astype(F32) + r2[...].astype(F32) + r3[...].astype(F32)
        unit_rows, scale = unit(middle_ref[...])
        live = live_rows(got_ref, slots, count)
        cot = cot_ref[...].astype(F32) * live
        grad = cot + norm_back(cotangent, small_ref[1:2], unit_rows, scale)
        grad_out[...] = grad
        branch = grad.astype(LOW)
        branch_out[...] = branch
        sums_out[0:1] = jnp.sum(cotangent * unit_rows, axis=0, keepdims=True)
        sums_out[1:2] = jnp.sum(cotangent, axis=0, keepdims=True)
        sums_out[2:3] = jnp.sum(branch.astype(F32), axis=0, keepdims=True)
        sums_out[3:4] = jnp.sum(cot, axis=0, keepdims=True)

    model = own.shape[1]
    shapes = [((slots, model), F32), ((slots, model), LOW), ((4, model), F32)]
    return run(kernel, shapes, links.scalars, [own, *received, middle, got, out_grad, small])


def attn_back(
    links,
    grads,
    got,
    proj,
    weights,
    normed,
    qkv,
    probs,
    attended,
    sums,
    bias,
    slots,
    rows,
):
    model = normed.shape[1]
    heads = probs.shape[1]
    part = heads * HEAD_DIM
    line = links.line
    full = -(-rows // 16) * 16
    scale = HEAD_DIM**-0.5

    def kernel(scalar_ref, *refs):
        grad_ref, ins = refs[0], refs[1:5]
        p_ref, w_ref, normed_ref, qkv_ref, probs_ref, att_ref, sums_ref, bias_ref = refs[5:13]
        pieces = refs[13:15]
        own_out, *sent_out, scratch, grad_qkv, branch, cols = refs[15:]
        j = scalar_ref[2]
        for k in range(4):
            block = slice(k * slots, (k + 1) * slots)
            branch[block] = grad_ref[j ^ k]
            cols[block] = choose(
                j, [grad_ref[j ^ k, :, p * part : (p + 1) * part] for p in range(4)]
            )
        proj_rows = p_ref[pl.ds(pl.multiple_of(j * part, part), part), :]
        grad_att = back_mult(branch[...], proj_rows).astype(LOW)
        for k in range(4):
            block = slice(k * slots, (k + 1) * slots)
            for h in range(heads):
                at = h * HEAD_DIM
                query = qkv_ref[block, at : at + HEAD_DIM]
                keys = qkv_ref[block, part + at : part + at + HEAD_DIM]
                values = qkv_ref[block, 2 * part + at : 2 * part + at + HEAD_DIM]
                prob = probs_ref[k, h]
                cot = grad_att[block, at : at + HEAD_DIM]
                grad_probs = back_mult(cot, values)
                inner = jnp.sum(prob * grad_probs, axis=-1, keepdims=True)
                grad_scores = (prob * (grad_probs - inner)).astype(LOW)
                grad_qkv[block, at : at + HEAD_DIM] = (mult(grad_scores, keys) * scale).astype(LOW)
                grad_qkv[block, part + at : part + at + HEAD_DIM] = (
                    contract(grad_scores, query) * scale
                ).astype(LOW)
                grad_qkv[block, 2 * part + at : 2 * part + at + HEAD_DIM] = contract(
                    prob.astype(LOW), cot
                ).astype(LOW)
        grad_rows = grad_qkv[...]
        qkv_sum = jnp.sum(grad_rows.astype(F32), axis=0, keepdims=True)
        grad_normed = back_mult(grad_rows, w_ref[:, : 3 * part])
        own_out[...] = grad_normed[:slots]
        for k in range(1, 4):
            sent_out[k - 1][...] = grad_normed[k * slots : (k + 1) * slots].astype(LOW)
        gain_sum = jnp.zeros((1, model), F32)
        for k in range(4):
            unit_rows = unit(ins[k][:slots].astype(F32))[0]
            block = slice(k * slots, (k + 1) * slots)
            gain_sum = gain_sum + jnp.sum(grad_normed[block] * unit_rows, axis=0, keepdims=True)
        shift_sum = jnp.sum(grad_normed, axis=0, keepdims=True)
        total = jnp.concatenate(
            [contract(normed_ref[...], grad_rows), contract(att_ref[...], cols[...])], axis=1
        )
        store_pieces(scalar_ref, scratch, total, pieces, 0)
        spread = lambda v: jnp.concatenate(
            [jnp.where(j == p, v, jnp.zeros_like(v)) for p in range(4)], axis=1
        )
        vectors = jnp.concatenate(
            [
                gain_sum,
                sums_ref[0:1],
                shift_sum,
                sums_ref[1:2],
                spread(qkv_sum[:, :part]),
                spread(qkv_sum[:, 2 * part :]),
                sums_ref[2:4],
                bias_ref[...],
                jnp.zeros((7, model), F32),
            ]
        ).astype(LOW)
        for out in pieces:
            for hop in range(line):
                out[pl.ds(hop * (full + 16) + full, 16), :] = vectors

    shapes = [
        *[((line * (full + 16), model), LOW)] * 2,
        ((slots, model), F32),
        *[((slots, model), LOW)] * 3,
    ]
    args = [grads, *got, proj, weights, normed, qkv, probs, attended, sums, bias]
    scratch = [
        pltpu.VMEM((2 * line, rows, model), F32),
        pltpu.VMEM((4 * slots, 3 * part), LOW),
        pltpu.VMEM((4 * slots, model), LOW),
        pltpu.VMEM((4 * slots, part), LOW),
    ]
    return run(kernel, shapes, links.scalars, args, scratch)


def ff_results(links, parts, rows):
    model = parts[0].shape[1]
    shards = links.shards
    full = -(-rows // 16) * 16

    def kernel(scalar_ref, *refs):
        ins, fc_out, fc2_out = refs[:4], refs[4], refs[5]
        j = scalar_ref[2]
        for p in range(4):
            left = choose(j ^ p, [ref[pl.ds(0, rows), :] for ref in ins]).astype(F32)
            for s in range(shards):
                at = (s * 4 + p) * rows
                fc_out[:, at : at + rows] = left[:, s * rows : (s + 1) * rows]
            fc2_out[pl.ds(p * rows, rows), :] = choose(
                j ^ p, [ref[pl.ds(full, rows), :] for ref in ins]
            ).astype(F32)

    shapes = [((rows, 4 * model), F32), ((4 * rows, model), F32)]
    return run(kernel, shapes, links.scalars, parts)


def attn_results(links, got, rows):
    model = got.shape[2]
    shards = links.shards
    part = model // 4
    full = -(-rows // 16) * 16

    def kernel(scalar_ref, *refs):
        got_ref, qkv_out, proj_out, gains_out, shifts_out, bias_out = refs
        s_here = scalar_ref[3]
        for p in range(4):
            block = got_ref[p, pl.ds(0, rows), :].astype(F32)
            for t in range(3):
                at = t * model + p * part
                qkv_out[:, at : at + part] = block[:, t * part : (t + 1) * part]
            proj_out[:, p * part : (p + 1) * part] = block[:, 3 * part :]
        cut = lambda v: choose(s_here, [v[:, s * rows : (s + 1) * rows] for s in range(shards)])
        low = [cut(got_ref[p, pl.ds(full, 16), :].astype(F32)) for p in range(4)]
        sums = low[0] + low[1] + low[2] + low[3]
        gains_out[...] = sums[:2]
        shifts_out[...] = sums[2:8]
        bias = jnp.concatenate([v[8:9] for v in low], axis=1)
        bias_out[...] = bias.reshape(bias_out.shape)

    shapes = [
        ((rows, 3 * model), F32),
        ((rows, model), F32),
        ((2, rows), F32),
        ((6, rows), F32),
        ((4 * rows,), F32),
    ]
    return run(kernel, shapes, links.scalars, [got])


def local(tokens, out_grad, lengths, gains, shifts, w_qkv, w_proj, w_fc, bias_fc, w_fc2):
    links = Links()
    line, shards = links.line, links.shards
    z, c, j = links.z, links.c, links.j
    slots, model = tokens.shape
    count = lengths.shape[1]
    rows = w_proj.shape[0]
    quarter = w_fc2.shape[0] // 4
    assert quarter == rows and w_fc.shape[1] == 4 * model
    heads = model // HEAD_DIM // 4
    part = heads * HEAD_DIM
    full_rows = -(-rows // 16) * 16

    attn_block = pack_attn(links, [gains, shifts, bias_fc, w_qkv, w_proj], rows, part, full_rows)
    sent = pack_slots(links, tie(tokens, attn_block), lengths)
    w_fc, w_fc2 = tie((w_fc, w_fc2), sent)
    ff_block = pack_ff(links, w_fc, w_fc2, rows, full_rows)

    attn_mine = line_gather(links, attn_block)
    got = links.rep_gather(sent)
    attn_mine, got, ff_block = lax.optimization_barrier((attn_mine, got, ff_block))
    attn_blocks = with_partners(links, attn_mine)
    ff_mine = line_gather(links, ff_block, links.line - 1)

    proj_mine, proj_other = proj_lanes(links, attn_blocks, out_grad, rows, part)
    proj = links.rep_gather(proj_mine)
    ff_own_theirs = links.core(ff_block)
    attn_blocks = tie(attn_blocks, (proj_mine, ff_own_theirs))
    weights, normed_one, qkv, probs, sent, small_f = attn_forward(
        links, got, attn_blocks, slots, heads, count, rows
    )
    ff_mine.append(links.along(tie(ff_block, sent), line - 1))
    attended = lax.all_gather(sent, "rep", axis=0)
    proj, ff_mine = tie((proj, ff_mine), attended)
    proj = proj + [proj_other] + [links.core(v) for v in proj[1:]]
    ff_blocks = with_partners(links, ff_mine, ff_own_theirs)
    (
        attended,
        middle,
        normed_two,
        active,
        grad_hidden,
        cot,
        own,
        sent_x,
        sent_y,
        sent_d,
        bias_sums,
        proj,
        fc2,
    ) = ff_both(links, got, attended, proj, ff_blocks, small_f, slots, count, rows)
    received = [links.rep(v, k) for k, v in ((1, sent_x), (2, sent_y), (3, sent_d))]
    ff_mine, ff_other, branch, sent_x, sent_y, sent_d = ff_grads(
        links, normed_two, active, grad_hidden, cot, fc2, slots, rows
    )
    branch_sent = [sent_x, sent_y, sent_d]
    ff_other = tie(ff_other, received)
    ff_theirs = links.core(ff_other)
    ff_sent, ff_own = line_sum(line, ff_mine, ff_theirs)
    grad_middle, grad_branch, sums = middle_back(
        links, own, received, middle, got[0], out_grad, small_f, slots, count
    )
    ff_sent = tie(ff_sent, grad_branch)
    branch_got = [links.rep(v, k) for k, v in enumerate(branch_sent, start=1)]
    grad_branch = tie(grad_branch, branch_got)
    grad_branch = lax.all_gather(grad_branch, "rep", axis=0)
    ff_sum = line_send(links, ff_sent, ff_own)

    attn_mine, attn_other, own, sent_x, sent_y, sent_d = attn_back(
        links,
        grad_branch,
        got,
        proj,
        weights,
        normed_one,
        qkv,
        probs,
        attended,
        sums,
        bias_sums,
        slots,
        rows,
    )
    attn_other = tie(attn_other, ff_sum)
    attn_theirs = links.core(attn_other)
    attn_sent, attn_own = line_sum(line, attn_mine, attn_theirs)
    attn_sent = tie(attn_sent, ff_sum)
    attn_sum = line_send(links, attn_sent, attn_own)

    own_sent = [sent_x, sent_y, sent_d]
    own_got = []
    for k in range(1, 4):
        own_got.append(links.rep(own_sent[k - 1], k))
        own = own + own_got[-1].astype(F32)
        branch = branch + branch_got[k - 1].astype(F32)
    live = (jnp.arange(slots) < jnp.sum(lengths)).astype(F32)[:, None]
    mixed_out = ((middle + branch + small_f[7]) * live).astype(LOW)
    unit_rows, scale = unit(tokens.astype(F32))
    grad_tokens = grad_middle + norm_back(own, small_f[0], unit_rows, scale)

    fc_out, fc2_out = ff_results(links, links.rep_gather(tie(ff_sum.astype(LOW), own_got)), rows)
    qkv_out, proj_out, gains_out, shifts_out, bias_out = attn_results(
        links, lax.all_gather(attn_sum.astype(LOW), "rep", axis=0), rows
    )
    return (
        mixed_out,
        grad_tokens,
        gains_out,
        shifts_out,
        qkv_out,
        proj_out,
        fc_out,
        bias_out,
        fc2_out,
    )


def solution(mesh):
    return jax.shard_map(
        local,
        mesh=mesh,
        in_specs=(
            P(("rep", "shard"), None),
            P(("rep", "shard"), None),
            P(("rep", "shard"), None),
            P(None, "shard"),
            P(None, "shard"),
            P("shard", None),
            P("shard", None),
            P("shard", None),
            P("shard"),
            P("shard", None),
        ),
        out_specs=(
            P(("rep", "shard"), None),
            P(("rep", "shard"), None),
            P(None, "shard"),
            P(None, "shard"),
            P("shard", None),
            P("shard", None),
            P("shard", None),
            P("shard"),
            P("shard", None),
        ),
        check_vma=False,
    )
```
